256 devices in a mesh: ctx: 64 (over x, y_hi, z), head: 4 (over y_lo, core).
Axes of the slice: x: 4, y: 4 (y_hi: 2, y_lo: 2; y = y_hi * 2 + y_lo), z: 8, core: 2. Of those that a mesh axis runs over, the one named last changes fastest.
Arguments:
- tokens: bfloat16 [8192, 1536], P('ctx', 'head'), may hold values from -6 to 6
- tissue: int32 [8192], P('ctx'), may hold values from 0 to 1, as said below
- conv_taps: float32 [83, 1536], P(None, 'head'), may hold values from -0.625 to 0.625
- conv_bias: float32 [1536], P('head'), may hold values from -3 to 3
- ln_gain: float32 [1536], replicated, may hold values from 0.5 to 2
- w_qkv: bfloat16 [1536, 3, 1024], P(None, None, 'head'), may hold values from -4 to 4
- w_out: bfloat16 [1024, 1536], P('head'), may hold values from -0.75 to 0.75
- drop_seed: int32 [2], replicated, may hold values from 0 to 1048575
- grad_out: bfloat16 [8192, 1536], P('ctx', 'head'), may hold values from -6 to 6
Outputs:
- encoded: bfloat16 [8192, 1536], P('ctx', 'head')
- grad_tokens: bfloat16 [8192, 1536], P('ctx', 'head')
The draws below stay inside these ranges and needn't reach their ends.
Inputs may be any that keep to these rules, and one draw needn't show every extreme that they name: The tissue tiles of each grid row of 32 columns form one run of columns, and every grid row holds at least one tissue tile. `drop_seed`: element 0 is the dropout seed, element 1 the key counter.
All inputs are finite; a program needn't handle non-finite values.
Results may differ from the reference program's by a relative error of at most 0.039.
Values may be sent and summed in bfloat16 or wider, within the bound.
A program may use at most 128 MiB of HBM per device.

```python
import math
import jax
import jax.numpy as jnp
from jax import lax

D = 1536
HEADS = 16
HEAD_DIM = 64
GRID_COLS = 32
TOK_DEV = 128
ATT_WIDTH = 1024
TOKENS = 8192


def draw_tissue(key, part):
    key = jax.random.fold_in(key, 17)
    band_key, width_key, center_key = jax.random.split(key, 3)
    grid_rows = TOKENS // GRID_COLS
    band_reach = jax.random.randint(band_key, (TOKENS // TOK_DEV,), 1, GRID_COLS // 2 + 1)
    row_reach = jnp.repeat(band_reach, TOK_DEV // GRID_COLS)
    half_width = 1 + jax.random.randint(width_key, (grid_rows,), 0, 1 << 20) % row_reach
    center = jax.random.randint(center_key, (grid_rows,), 0, GRID_COLS)
    columns = jnp.arange(GRID_COLS)[None, :]
    alive = jnp.abs(columns - center[:, None]) < half_width[:, None]
    return alive.astype(jnp.int32).reshape(TOKENS)


def draw_w_qkv(key, part):
    key = jax.random.fold_in(key, 29)
    base_key = jax.random.fold_in(key, 0)
    width = HEADS * HEAD_DIM
    base = jax.random.normal(base_key, (D, 3, width), jnp.float32) * (1.25 / jnp.sqrt(jnp.float32(D)))
    return jnp.clip(base, -4.0, 4.0).astype(jnp.bfloat16)


def block_scale(stream_key, shape, pieces, low, high):
    level = 1.0
    for dim, parts in pieces:
        steps = jax.random.uniform(jax.random.fold_in(jax.random.fold_in(stream_key, 6), dim), (parts,), jnp.float32, low / len(pieces), high / len(pieces))
        level = level * jnp.repeat(jnp.exp(steps), shape[dim] // parts).reshape((-1,) + (1,) * (len(shape) - 1 - dim))
    return level


def bell_draw(stream_key, extent, scale, bound, shards=(), kind=jnp.bfloat16):
    result = scale * jax.random.normal(stream_key, extent, jnp.float32)
    if shards:
        result = result * block_scale(stream_key, extent, shards, -0.22, 0.18)
    return jnp.clip(result, -bound, bound).astype(kind)


def setup_inputs(seed: int = 0) -> dict:
    key_list = jax.random.split(jax.random.key(seed), 10)
    return {
        "tokens": bell_draw(key_list[0], (TOKENS, D), 1.0, 6.0, ((0, 64), (1, 4))),
        "tissue": draw_tissue(jax.random.fold_in(key_list[9], 71), 0),
        "conv_taps": bell_draw(key_list[2], (83, D), 83 ** -0.5, 0.625, ((1, 4),), jnp.float32),
        "conv_bias": bell_draw(key_list[3], (D,), 0.5, 3.0, ((0, 4),), jnp.float32),
        "ln_gain": jnp.clip(jnp.exp(jax.random.uniform(key_list[4], (D,), jnp.float32, math.log(0.5), math.log(2.0))), 0.5, 2.0),
        "w_qkv": draw_w_qkv(jax.random.fold_in(key_list[9], 71), 0),
        "w_out": bell_draw(key_list[6], (ATT_WIDTH, D), (ATT_WIDTH // 16) ** -0.5, 0.75, ((0, 4),)),
        "drop_seed": jax.random.randint(key_list[7], (2,), 0, 1048576).astype(jnp.int32),
        "grad_out": bell_draw(key_list[8], (TOKENS, D), 1.0, 6.0, ((0, 64), (1, 4))),
    }


DROP_LEVEL = 103
KEEP_SCALE = 1024.0 / 921.0
NEG = -1e+30
EPS = 1e-05

def keep_mask(anchor, counter, row_ids, col_ids):
    mixed = row_ids * jnp.int32(374761393) + col_ids * jnp.int32(668265263) + anchor * jnp.int32(1274126177) + counter
    mixed = jnp.bitwise_xor(mixed, lax.shift_right_logical(mixed, jnp.full_like(mixed, 15)))
    mixed = mixed * jnp.int32(16777619)
    mixed = jnp.bitwise_xor(mixed, lax.shift_right_logical(mixed, jnp.full_like(mixed, 13)))
    mixed = mixed * jnp.int32(1274126177)
    mixed = jnp.bitwise_xor(mixed, lax.shift_right_logical(mixed, jnp.full_like(mixed, 16)))
    return (jnp.bitwise_and(mixed, jnp.int32(1023)) >= DROP_LEVEL).astype(jnp.float32)

def depthwise(field, conv_taps, flipped):
    grid_rows, grid_cols = (field.shape[0], field.shape[1])
    padded = jnp.pad(field, ((3, 3), (3, 3), (0, 0)))
    total = jnp.zeros_like(field)
    offset = 0
    for size in (7, 5, 3):
        half = size // 2
        for row_off in range(size):
            for col_off in range(size):
                weight = conv_taps[offset + row_off * size + col_off]
                if flipped:
                    upper = 3 + half - row_off
                    left = 3 + half - col_off
                else:
                    upper = 3 - half + row_off
                    left = 3 - half + col_off
                total = total + weight * padded[upper:upper + grid_rows, left:left + grid_cols]
        offset += size * size
    return total

def blocks_of(array, block):
    return array.reshape((array.shape[0] // block, block) + array.shape[1:])

def reference(tokens, tissue, conv_taps, conv_bias, ln_gain, w_qkv, w_out, drop_seed, grad_out):
    total_rows, model_width = tokens.shape
    att_width = w_out.shape[0]
    heads = att_width // HEAD_DIM
    scale_factor = 1.0 / math.sqrt(HEAD_DIM)
    alive_col = tissue.astype(jnp.float32)[:, None]
    usable = (tissue > 0)[None, None, :]
    grid_shape = (total_rows // GRID_COLS, GRID_COLS, model_width)
    masked = tokens * tissue.astype(jnp.bfloat16)[:, None]
    masked32 = masked.astype(jnp.float32)
    mixed = depthwise(masked32.reshape(grid_shape), conv_taps, False).reshape(total_rows, model_width)
    residual = ((masked32 + conv_bias + mixed) * alive_col).astype(jnp.bfloat16)
    stream = residual.astype(jnp.float32)
    center = stream - lax.optimization_barrier(jnp.mean(stream, axis=-1, keepdims=True))
    spread = lax.rsqrt(lax.optimization_barrier(jnp.mean(center * center, axis=-1, keepdims=True)) + EPS)
    unit = center * spread
    normed = (unit * ln_gain).astype(jnp.bfloat16)
    flat_w = w_qkv.reshape(model_width, 3 * att_width)
    project = jnp.dot(normed, flat_w, preferred_element_type=jnp.float32).astype(jnp.bfloat16)
    project = project.reshape(total_rows, 3, heads, HEAD_DIM).astype(jnp.float32)
    queries, keys, values = (project[:, 0], project[:, 1], project[:, 2])
    block = math.gcd(total_rows, 256)

    def forward_rows(query_block):
        scores = jnp.einsum('qhd,khd->hqk', query_block, keys) * scale_factor
        scores = jnp.where(usable, scores, NEG)
        highest = lax.optimization_barrier(jnp.max(scores, axis=-1))
        weights = jnp.where(usable, jnp.exp(scores - highest[..., None]), 0.0)
        totals = lax.optimization_barrier(jnp.sum(weights, axis=-1))
        summed = jnp.einsum('hqk,khd->qhd', weights.astype(jnp.bfloat16).astype(jnp.float32), values)
        return (summed / totals.T[..., None], (highest + jnp.log(totals)).T)
    attended, log_total = lax.map(forward_rows, blocks_of(queries, block))
    attended = attended.reshape(total_rows, heads, HEAD_DIM).astype(jnp.bfloat16)
    log_total = log_total.reshape(total_rows, heads)
    branch = jnp.dot(attended.reshape(total_rows, att_width), w_out, preferred_element_type=jnp.float32)
    row_ids = lax.iota(jnp.int32, total_rows)[:, None]
    col_ids = lax.iota(jnp.int32, model_width)[None, :]
    keep = keep_mask(drop_seed[0], drop_seed[1], row_ids, col_ids)
    encoded = ((stream + branch * keep * KEEP_SCALE) * alive_col).astype(jnp.bfloat16)
    upstream = grad_out.astype(jnp.float32) * alive_col
    drop_grad = (upstream * keep * KEEP_SCALE).astype(jnp.bfloat16)
    out_grad = jnp.dot(drop_grad, w_out.T, preferred_element_type=jnp.float32).astype(jnp.bfloat16)
    out_grad = out_grad.reshape(total_rows, heads, HEAD_DIM).astype(jnp.float32)
    shift = lax.optimization_barrier(jnp.sum(out_grad * attended.astype(jnp.float32), axis=-1))

    def query_rows(inputs):
        query_block, grad_block, log_block, shift_block = inputs
        scores = jnp.einsum('qhd,khd->hqk', query_block, keys) * scale_factor
        probs = jnp.where(usable, jnp.exp(scores - log_block.T[..., None]), 0.0)
        dprob = jnp.einsum('qhd,khd->hqk', grad_block, values)
        slope = (probs * (dprob - shift_block.T[..., None]) * scale_factor).astype(jnp.bfloat16).astype(jnp.float32)
        return jnp.einsum('hqk,khd->qhd', slope, keys)
    query_grad = lax.map(query_rows, (blocks_of(queries, block), blocks_of(out_grad, block), blocks_of(log_total, block), blocks_of(shift, block)))
    query_grad = query_grad.reshape(total_rows, heads, HEAD_DIM)

    def key_rows(inputs):
        key_block, value_block, alive_block = inputs
        usable_block = (alive_block > 0)[None, None, :]
        scores = jnp.einsum('qhd,khd->hqk', queries, key_block) * scale_factor
        probs = jnp.where(usable_block, jnp.exp(scores - log_total.T[..., None]), 0.0)
        dprob = jnp.einsum('qhd,khd->hqk', out_grad, value_block)
        slope = (probs * (dprob - shift.T[..., None]) * scale_factor).astype(jnp.bfloat16).astype(jnp.float32)
        key_grad = jnp.einsum('hqk,qhd->khd', slope, queries)
        value_grad = jnp.einsum('hqk,qhd->khd', probs.astype(jnp.bfloat16).astype(jnp.float32), out_grad)
        return (key_grad, value_grad)
    key_grad, value_grad = lax.map(key_rows, (blocks_of(keys, block), blocks_of(values, block), blocks_of(tissue, block)))
    key_grad = key_grad.reshape(total_rows, heads, HEAD_DIM)
    value_grad = value_grad.reshape(total_rows, heads, HEAD_DIM)
    grads = jnp.stack([query_grad, key_grad, value_grad], axis=1).astype(jnp.bfloat16).reshape(total_rows, 3 * att_width)
    normed_grad = jnp.dot(grads, flat_w.T, preferred_element_type=jnp.float32)
    scaled = normed_grad * ln_gain
    inner = scaled - lax.optimization_barrier(jnp.mean(scaled, axis=-1, keepdims=True)) - unit * lax.optimization_barrier(jnp.mean(scaled * unit, axis=-1, keepdims=True))
    layer_grad = inner * spread
    source_grad = ((upstream + layer_grad) * alive_col).astype(jnp.bfloat16)
    source32 = source_grad.astype(jnp.float32)
    spread_back = depthwise(source32.reshape(grid_shape), conv_taps, True).reshape(total_rows, model_width)
    grad_tokens = ((source32 + spread_back) * alive_col).astype(jnp.bfloat16)
    return (encoded, grad_tokens)
```

```python
import jax
import jax.numpy as jnp
from jax import lax
from jax.experimental import pallas as pl
from jax.experimental.pallas import tpu as pltpu
from jax.sharding import PartitionSpec as P

HEAD_DIM = 64
GRID_COLS = 32
ROWS = 128
QUADS = 4
BLOCKS = 16
SPAN = BLOCKS * ROWS
CHUNK = 256
HALF = ROWS // 2
WHOLE = 60 << 20

DROP_LEVEL = 103
KEEP_SCALE = 1024.0 / 921.0
NEG = -1e30
EPS = 1e-05
DEAD = 2.0**100

MESH = pl.DeviceIdType.MESH
ANY = pl.BlockSpec(memory_space=pl.ANY)
NT = (((1,), (1,)), ((), ()))


def struct(shape, dtype=jnp.bfloat16):
    return jax.ShapeDtypeStruct(shape, dtype)


def place():
    ctx = lax.axis_index("ctx")
    return ctx, ctx // 16, (ctx // 8) % 2, ctx % 8


def query_peers():
    ctx, x, y, z = place()
    mine = ctx % 16
    peers = []
    for step in range(1, 16):
        to = (mine + step) % 16
        peers.append((x * 16 + to, to, 2 * (to // 8) + to % 2))
    return mine, 2 * y + z % 2, peers


def key_peers():
    ctx, x, y, z = place()
    mine = x * 4 + y * 2 + z % 2
    peers = []
    for step in range(1, 16):
        to = (mine + step) % 16
        peers.append((((to // 4) * 2 + (to // 2) % 2) * 8 + (z // 2) * 2 + to % 2, to, to % 4))
    return mine, 2 * y + z % 2, peers


def stat_peers():
    ctx, x, y, z = place()
    mine = z // 2
    peers = []
    for step in range(1, 4):
        to = (mine + step) % 4
        peers.append(((ctx // 8) * 8 + to * 2 + z % 2, to))
    return mine, peers


def head_peers():
    mine = lax.axis_index("head")
    return mine, [(mine + step) % 4 for step in range(1, 4)]


class Copies:
    def __init__(self, send, recv, own):
        self.send, self.recv, self.own = send, recv, own
        self.far, self.near = [], []

    def to(self, src, dst, device):
        at = len(self.far)
        copy = pltpu.make_async_remote_copy(
            src_ref=src,
            dst_ref=dst,
            send_sem=self.send.at[at],
            recv_sem=self.recv.at[at],
            device_id=device,
            device_id_type=MESH,
        )
        copy.start()
        self.far.append(copy)
        return copy

    def here(self, src, dst):
        copy = pltpu.make_async_copy(src, dst, self.own.at[len(self.near)])
        copy.start()
        self.near.append(copy)
        return copy

    def sent(self):
        for copy in self.far:
            copy.wait_send()


def received(copies):
    for copy in copies:
        copy.wait_recv()


def ring_ids():
    ctx = lax.axis_index("ctx")
    return (ctx + 63) % 64, (ctx + 1) % 64


def everyone():
    before, after = ring_ids()
    ids = [{"ctx": before}, {"ctx": after}]
    ids += [{"head": h} for h in head_peers()[1]]
    ids += [{"ctx": c} for c, _, _ in query_peers()[2]]
    return ids + [{"ctx": c} for c, _, _ in key_peers()[2]]


def announce(ids):
    barrier = pltpu.get_barrier_semaphore()
    for device in ids:
        pl.semaphore_signal(barrier, inc=1, device_id=device, device_id_type=MESH)


def all_here(ids):
    pl.semaphore_wait(pltpu.get_barrier_semaphore(), len(ids))


def stat_kernel(stats, stats_all, send, recv, own):
    mine, peers = stat_peers()
    ids = [{"ctx": c} for c, _ in peers]
    announce(ids)
    copies = Copies(send, recv, own)
    kept = copies.here(stats.at[pl.ds(0, 32)], stats_all.at[mine])
    all_here(ids)
    for device in ids:
        copies.to(stats.at[pl.ds(0, 32)], stats_all.at[mine], device)
    kept.wait()
    received(copies.far)
    copies.sent()


def lanes(rows, width=128):
    return lax.broadcasted_iota(jnp.int32, (rows, width), 1)


def normalised(full_ref):
    parts = [full_ref[i].astype(jnp.float32) for i in range(QUADS)]
    width = QUADS * parts[0].shape[1]
    mean = sum(jnp.sum(p, axis=1, keepdims=True) for p in parts) / width
    parts = [p - mean for p in parts]
    var = sum(jnp.sum(p * p, axis=1, keepdims=True) for p in parts) / width
    spread = lax.rsqrt(var + EPS)
    return [p * spread for p in parts], spread


def fold(top, bottom, low_half):
    low = lanes(top.shape[0]) < HEAD_DIM
    if low_half:
        return jnp.where(low, top, pltpu.roll(bottom, 64, 1))
    return jnp.where(low, pltpu.roll(top, 64, 1), bottom)


def fold_rows(block, low_half):
    return fold(block[0:64], block[64:128], low_half)


def unfold_rows(packed, low_half):
    moved = pltpu.roll(packed, 64, 1)
    return jnp.concatenate([packed, moved] if low_half else [moved, packed], axis=0)


def query_block(q_ref, d_ref, at):
    q = unfold_rows(q_ref[at].astype(jnp.float32), False)
    d = unfold_rows(d_ref[at].astype(jnp.float32), True)
    return jnp.where(lanes(ROWS) < HEAD_DIM, d, q)


def build_keys(vk_ref, keys):
    for block in range(BLOCKS):
        rows = slice(block * ROWS, (block + 1) * ROWS)
        part = vk_ref[block].astype(jnp.float32)
        dead = part[:, 0:1] > DEAD / 2
        lane = lanes(ROWS)
        bias = jnp.where(dead, NEG, 0.0)
        aux = jnp.where(lane == 0, bias, jnp.where(lane < 4, 1.0, 0.0))
        keys[rows, 0:128] = jnp.where(dead, 0.0, part).astype(jnp.bfloat16)
        keys[rows, 128:256] = aux.astype(jnp.bfloat16)


def query_chunk(q_ref, d_ref):
    return jnp.concatenate([query_block(q_ref, d_ref, i) for i in range(CHUNK // ROWS)], axis=0)


def forward_kernel(q_ref, d_ref, vk_ref, p_ref, o_ref, stat_ref, keys):
    step = pl.program_id(0)

    @pl.when(step == 0)
    def _():
        build_keys(vk_ref, keys)

    q = query_chunk(q_ref, d_ref)
    lane = lanes(CHUNK)
    left = jnp.concatenate(
        [jnp.where(lane >= HEAD_DIM, q * 0.125, 0.0), jnp.where(lane == 0, 1.0, 0.0)], axis=1
    ).astype(jnp.bfloat16)
    scores = lax.dot_general(left, keys[...], NT, preferred_element_type=jnp.float32)
    highest = jnp.max(scores, axis=1, keepdims=True)
    weights = jnp.exp(scores - highest).astype(jnp.bfloat16)
    p_ref[...] = weights
    summed = jnp.dot(weights, keys[...], preferred_element_type=jnp.float32)
    totals = summed[:, 129:130]
    attended = summed[:, 0:128] / totals
    o_ref[...] = attended
    inner = jnp.sum(jnp.where(lane < HEAD_DIM, attended * q, 0.0), axis=1, keepdims=True)
    log_total = highest + jnp.log(totals)
    table = jnp.where(
        lane == 0, log_total, jnp.where(lane == 1, inner, jnp.where(lane == 2, highest, 0.0))
    ).T
    for kind in range(3):
        for half in range(2):
            stat_ref[pl.ds(16 * kind + 2 * step + half, 1), :] = table[
                kind : kind + 1, half * 128 : half * 128 + 128
            ]


def backward_kernel(
    q_ref,
    d_ref,
    vk_ref,
    p_ref,
    o_ref,
    stat_ref,
    stats_ref,
    out_ref,
    query_ref,
    grad_ref,
    keys,
    table,
    value_acc,
    key_acc,
):
    step = pl.program_id(0)

    @pl.when(step == 0)
    def _():
        build_keys(vk_ref, keys)
        value_acc[...] = jnp.zeros_like(value_acc)
        key_acc[...] = jnp.zeros_like(key_acc)
        logs = [stats_ref[i, 0:16, :] for i in range(4)]
        top = jnp.maximum(jnp.maximum(logs[0], logs[1]), jnp.maximum(logs[2], logs[3]))
        total = top + jnp.log(sum(jnp.exp(part - top) for part in logs))
        shift = sum(jnp.exp(logs[i] - total) * stats_ref[i, 16:32, :] for i in range(4))
        share = jnp.exp(stat_ref[0:16, :] - total)
        factor = jnp.exp(stat_ref[32:48, :] - total)
        rows = jnp.concatenate([share, shift, factor, jnp.zeros((80, 128), jnp.float32)], axis=0)
        table[...] = rows.T

    lane = lanes(ROWS)

    def column(kind):
        return jnp.concatenate(
            [
                jnp.sum(
                    jnp.where(lane == 16 * kind + 2 * step + half, table[...], 0.0),
                    axis=1,
                    keepdims=True,
                )
                for half in range(2)
            ],
            axis=0,
        )

    share, shift, factor = column(0), column(1), column(2)
    lane = lanes(CHUNK)
    qd = query_chunk(q_ref, d_ref)
    high = shift.astype(jnp.bfloat16).astype(jnp.float32)
    middle = (shift - high).astype(jnp.bfloat16).astype(jnp.float32)
    low = shift - high - middle
    extra = jnp.where(
        lane == 1, -high, jnp.where(lane == 2, -middle, jnp.where(lane == 3, -low, 0.0))
    )
    left = jnp.concatenate([jnp.where(lane < HEAD_DIM, qd, 0.0), extra], axis=1).astype(
        jnp.bfloat16
    )
    dprob = lax.dot_general(left, keys[...], NT, preferred_element_type=jnp.float32)
    weights = p_ref[...]
    slope = (weights.astype(jnp.float32) * dprob).astype(jnp.bfloat16)
    query_grad = jnp.dot(slope, keys[:, 0:128], preferred_element_type=jnp.float32)
    query_grad = query_grad * (factor * 0.125)
    attended = o_ref[...] * share
    for block in range(CHUNK // ROWS):
        rows = slice(block * ROWS, (block + 1) * ROWS)
        query_ref[block] = fold_rows(query_grad[rows], False).astype(jnp.bfloat16)
        out_ref[block] = fold_rows(attended[rows], True).astype(jnp.bfloat16)
    scaled = (qd * factor * jnp.where(lane < HEAD_DIM, 1.0, 0.125)).T.astype(jnp.bfloat16)
    value_acc[...] += jnp.dot(scaled[0:64], weights, preferred_element_type=jnp.float32)
    key_acc[...] += jnp.dot(scaled[64:128], slope, preferred_element_type=jnp.float32)

    @pl.when(step == pl.num_programs(0) - 1)
    def _():
        for block in range(BLOCKS):
            cols = slice(block * ROWS, (block + 1) * ROWS)
            both = jnp.concatenate([value_acc[:, cols], key_acc[:, cols]], axis=0)
            grad_ref[block] = both.T.astype(jnp.bfloat16)


def attention_forward(query_all, grad_all, key_all):
    per = CHUNK // ROWS
    return pl.pallas_call(
        forward_kernel,
        grid=(SPAN // CHUNK,),
        in_specs=[
            pl.BlockSpec((per, HALF, 128), lambda i: (i, 0, 0)),
            pl.BlockSpec((per, HALF, 128), lambda i: (i, 0, 0)),
            pl.BlockSpec((BLOCKS, ROWS, 128), lambda i: (0, 0, 0)),
        ],
        out_specs=[
            pl.BlockSpec((CHUNK, SPAN), lambda i: (i, 0)),
            pl.BlockSpec((CHUNK, 128), lambda i: (i, 0)),
            pl.BlockSpec((48, 128), lambda i: (0, 0)),
        ],
        out_shape=[
            struct((SPAN, SPAN)),
            struct((SPAN, 128), jnp.float32),
            struct((48, 128), jnp.float32),
        ],
        scratch_shapes=[pltpu.VMEM((SPAN, 256), jnp.bfloat16)],
        compiler_params=pltpu.CompilerParams(vmem_limit_bytes=WHOLE),
    )(query_all, grad_all, key_all)


def attention_backward(query_all, grad_all, key_all, weights, attended, stat, stats):
    per = CHUNK // ROWS
    return pl.pallas_call(
        backward_kernel,
        grid=(SPAN // CHUNK,),
        in_specs=[
            pl.BlockSpec((per, HALF, 128), lambda i: (i, 0, 0)),
            pl.BlockSpec((per, HALF, 128), lambda i: (i, 0, 0)),
            pl.BlockSpec((BLOCKS, ROWS, 128), lambda i: (0, 0, 0)),
            pl.BlockSpec((CHUNK, SPAN), lambda i: (i, 0)),
            pl.BlockSpec((CHUNK, 128), lambda i: (i, 0)),
            pl.BlockSpec((48, 128), lambda i: (0, 0)),
            pl.BlockSpec((4, 32, 128), lambda i: (0, 0, 0)),
        ],
        out_specs=[
            pl.BlockSpec((per, HALF, 128), lambda i: (i, 0, 0)),
            pl.BlockSpec((per, HALF, 128), lambda i: (i, 0, 0)),
            pl.BlockSpec((BLOCKS, ROWS, 128), lambda i: (0, 0, 0)),
        ],
        out_shape=[
            struct((BLOCKS, HALF, 128)),
            struct((BLOCKS, HALF, 128)),
            struct((BLOCKS, ROWS, 128)),
        ],
        scratch_shapes=[
            pltpu.VMEM((SPAN, 256), jnp.bfloat16),
            pltpu.VMEM((128, 128), jnp.float32),
            pltpu.VMEM((HEAD_DIM, SPAN), jnp.float32),
            pltpu.VMEM((HEAD_DIM, SPAN), jnp.float32),
        ],
        compiler_params=pltpu.CompilerParams(vmem_limit_bytes=WHOLE),
    )(query_all, grad_all, key_all, weights, attended, stat, stats)


def keep_mask(anchor, counter, row_ids, col_ids):
    mixed = (
        row_ids * jnp.int32(374761393)
        + col_ids * jnp.int32(668265263)
        + anchor * jnp.int32(1274126177)
        + counter
    )
    mixed = jnp.bitwise_xor(mixed, lax.shift_right_logical(mixed, jnp.full_like(mixed, 15)))
    mixed = mixed * jnp.int32(16777619)
    mixed = jnp.bitwise_xor(mixed, lax.shift_right_logical(mixed, jnp.full_like(mixed, 13)))
    mixed = mixed * jnp.int32(1274126177)
    mixed = jnp.bitwise_xor(mixed, lax.shift_right_logical(mixed, jnp.full_like(mixed, 16)))
    return (jnp.bitwise_and(mixed, jnp.int32(1023)) >= DROP_LEVEL).astype(jnp.float32)


def own_keep(seed_ref, rows, width):
    row_ids = lax.axis_index("ctx") * rows + lax.broadcasted_iota(jnp.int32, (rows, width), 0)
    col_ids = lax.axis_index("head") * width + lax.broadcasted_iota(jnp.int32, (rows, width), 1)
    return keep_mask(seed_ref[0], seed_ref[1], row_ids, col_ids)


def alive_column(tissue_ref):
    row = tissue_ref[...].astype(jnp.float32)
    return jnp.broadcast_to(row, (ROWS, ROWS)).T


def merged_tap(taps_ref, row, col, cols):
    tap = taps_ref[row * 7 + col : row * 7 + col + 1, cols]
    if 1 <= row <= 5 and 1 <= col <= 5:
        at = 49 + (row - 1) * 5 + col - 1
        tap = tap + taps_ref[at : at + 1, cols]
    if 2 <= row <= 4 and 2 <= col <= 4:
        at = 74 + (row - 2) * 3 + col - 2
        tap = tap + taps_ref[at : at + 1, cols]
    return tap


def depthwise(flipped, field, above, below, taps_ref, bias, alive, padded):
    ctx = lax.axis_index("ctx")
    width = field.shape[1]
    grid_rows = ROWS // GRID_COLS
    has_above = jnp.where(ctx > 0, 1.0, 0.0)
    has_below = jnp.where(ctx < 63, 1.0, 0.0)
    field = field.astype(jnp.float32)
    padded[:, 0:8, :] = jnp.zeros((grid_rows + 6, 8, width), jnp.float32)
    padded[:, 40:48, :] = jnp.zeros((grid_rows + 6, 8, width), jnp.float32)
    padded[0:3, 8:40, :] = (above.astype(jnp.float32) * has_above).reshape(3, GRID_COLS, width)
    padded[3:7, 8:40, :] = field.reshape(grid_rows, GRID_COLS, width)
    padded[7:10, 8:40, :] = (below.astype(jnp.float32) * has_below).reshape(3, GRID_COLS, width)
    for start in range(0, width, 128):
        cols = slice(start, start + 128)
        total = field[:, cols].reshape(grid_rows, GRID_COLS, 128)
        if bias is not None:
            total = total + bias[:, cols].reshape(1, 1, 128)
        for col in range(7):
            moved = padded[:, 5 + col : 37 + col, cols]
            for row in range(7):
                if flipped:
                    tap = merged_tap(taps_ref, 6 - row, 6 - col, cols)
                else:
                    tap = merged_tap(taps_ref, row, col, cols)
                total = total + tap.reshape(1, 1, 128) * moved[row : row + grid_rows]
        yield cols, total.reshape(ROWS, 128) * alive


def front_kernel(
    seed_ref,
    tokens_in,
    tissue_in,
    grad_in,
    taps_in,
    bias_in,
    gain_in,
    w_in,
    w_out_in,
    query_all,
    grad_all,
    key_all,
    full_all,
    tokens,
    tissue,
    grad,
    taps,
    bias,
    gain,
    w,
    w_out,
    masked,
    above,
    below,
    drop_full,
    full,
    query_part,
    grad_part,
    key_part,
    padded,
    send,
    recv,
    own,
):
    rows, width = tokens.shape
    ids = everyone()
    announce(ids)
    copies = Copies(send, recv, own)
    first = [
        copies.here(src, dst)
        for src, dst in ((tokens_in, tokens), (tissue_in, tissue), (grad_in, grad))
    ]
    for_conv = [copies.here(taps_in, taps), copies.here(bias_in, bias)]
    for_grad = [copies.here(w_out_in, w_out)]
    for_project = [copies.here(gain_in, gain), copies.here(w_in, w)]
    before, after = ring_ids()
    mine, heads = head_peers()
    keep = own_keep(seed_ref, rows, width)
    for copy in first:
        copy.wait()
    alive = alive_column(tissue)
    column = alive[:, 0:1]
    masked[...] = (tokens[...].astype(jnp.float32) * column).astype(jnp.bfloat16)
    all_here(ids)
    halos = [
        copies.to(masked.at[pl.ds(32, 96)], above, {"ctx": after}),
        copies.to(masked.at[pl.ds(0, 96)], below, {"ctx": before}),
    ]
    upstream = grad[...].astype(jnp.float32) * column
    drop_full[mine] = (upstream * keep * KEEP_SCALE).astype(jnp.bfloat16)
    drops = [copies.to(drop_full.at[mine], drop_full.at[mine], {"head": h}) for h in heads]

    for copy in for_conv:
        copy.wait()
    received(halos)
    for cols, part in depthwise(
        False, masked[...], above[...], below[...], taps, bias[...], alive, padded
    ):
        full[mine, :, cols] = part.astype(jnp.bfloat16)
    parts = [copies.to(full.at[mine], full.at[mine], {"head": h}) for h in heads]

    q_mine, slot, q_peers = query_peers()
    k_mine, _, k_peers = key_peers()
    for copy in for_grad:
        copy.wait()
    received(drops)
    out_grad = sum(
        lax.dot_general(
            drop_full[i],
            w_out[:, i * width : (i + 1) * width],
            NT,
            preferred_element_type=jnp.float32,
        )
        for i in range(QUADS)
    )
    for j in range(QUADS):
        pair = out_grad[:, 128 * (j // 2) : 128 * (j // 2) + 128]
        grad_part[j] = fold_rows(pair, j % 2 == 0).astype(jnp.bfloat16)
    landing = [
        copies.to(grad_part.at[h], grad_all.at[q_mine], {"ctx": c}) for c, _, h in q_peers
    ]
    local = [copies.here(grad_part.at[slot], grad_all.at[q_mine])]

    for copy in for_project:
        copy.wait()
    received(parts)
    local.append(copies.here(full, full_all))
    unit, _ = normalised(full)
    sums = [jnp.zeros((rows, w.shape[2]), jnp.float32) for _ in range(3)]
    for i in range(QUADS):
        span = slice(i * width, (i + 1) * width)
        normed = (unit[i] * gain[:, span]).astype(jnp.bfloat16)
        for k in range(3):
            sums[k] = sums[k] + jnp.dot(normed, w[k, span, :], preferred_element_type=jnp.float32)
    low = lanes(ROWS) < HEAD_DIM
    dead = alive == 0.0
    for j in range(QUADS):
        q, k, v = (part[:, 128 * (j // 2) : 128 * (j // 2) + 128] for part in sums)
        query_part[j] = fold_rows(q, j % 2 == 0).astype(jnp.bfloat16)
        if j % 2 == 0:
            both = jnp.where(low, v, pltpu.roll(k, 64, 1))
        else:
            both = jnp.where(low, pltpu.roll(v, 64, 1), k)
        key_part[j] = jnp.where(dead, DEAD, both).astype(jnp.bfloat16)
    for (qc, _, qh), (kc, _, kh) in zip(q_peers, k_peers):
        landing.append(copies.to(key_part.at[kh], key_all.at[k_mine], {"ctx": kc}))
        landing.append(copies.to(query_part.at[qh], query_all.at[q_mine], {"ctx": qc}))
    local.append(copies.here(query_part.at[slot], query_all.at[q_mine]))
    local.append(copies.here(key_part.at[slot], key_all.at[k_mine]))
    for copy in local:
        copy.wait()
    received(landing)
    copies.sent()


def back_kernel(
    seed_ref,
    attended_in,
    query_in,
    key_in,
    full_in,
    tissue_in,
    grad_in,
    taps_in,
    gain_in,
    w_in,
    w_out_in,
    encoded_out,
    tokens_out,
    tissue,
    grad,
    taps,
    gain,
    w,
    w_out,
    full,
    attended_all,
    query_all,
    key_all,
    grad_send,
    grad_recv,
    branch_send,
    branch_recv,
    sums_send,
    sums_recv,
    source,
    above,
    below,
    encoded,
    result,
    padded,
    send,
    recv,
    own,
):
    rows, width = grad.shape
    ids = everyone()
    announce(ids)
    copies = Copies(send, recv, own)
    q_mine, _, q_peers = query_peers()
    k_mine, _, k_peers = key_peers()
    first = [
        copies.here(src, dst)
        for src, dst in ((tissue_in, tissue), (grad_in, grad), (full_in, full), (gain_in, gain))
    ]
    later = [copies.here(src, dst) for src, dst in ((w_in, w), (w_out_in, w_out), (taps_in, taps))]
    kept = [
        copies.here(query_in.at[q_mine], query_all.at[q_mine]),
        copies.here(key_in.at[k_mine], key_all.at[k_mine]),
        copies.here(attended_in.at[q_mine], attended_all.at[q_mine]),
    ]
    all_here(ids)
    grads_back, outs_back = [], []
    for (qc, qd, _), (kc, kd, _) in zip(q_peers, k_peers):
        grads_back.append(copies.to(key_in.at[kd], key_all.at[k_mine], {"ctx": kc}))
        grads_back.append(copies.to(query_in.at[qd], query_all.at[q_mine], {"ctx": qc}))
    for qc, qd, _ in q_peers:
        outs_back.append(copies.to(attended_in.at[qd], attended_all.at[q_mine], {"ctx": qc}))

    mine, heads = head_peers()
    before, after = ring_ids()
    for copy in first + later:
        copy.wait()
    keep = own_keep(seed_ref, rows, width)
    alive = alive_column(tissue)
    column = alive[:, 0:1]
    unit, spread = normalised(full)
    low = lanes(ROWS) < HEAD_DIM

    def total(ref, slots):
        parts = [ref[s].astype(jnp.float32) for s in slots]
        return (parts[0] + parts[1]) + (parts[2] + parts[3])

    def queries(ref):
        heads_ = []
        for j in range(QUADS):
            packed = total(ref, [8 * (j // 2) + 2 * k + j % 2 for k in range(4)])
            heads_.append(unfold_rows(packed, j % 2 == 0))
        pairs = [jnp.where(low, heads_[2 * p], heads_[2 * p + 1]) for p in range(2)]
        return jnp.concatenate(pairs, axis=1).astype(jnp.bfloat16)

    for copy in kept:
        copy.wait()
    received(grads_back)
    both = [total(key_all, [4 * k + j for k in range(4)]) for j in range(QUADS)]
    values = [jnp.where(low, both[2 * p], pltpu.roll(both[2 * p + 1], 64, 1)) for p in range(2)]
    keys = [jnp.where(low, pltpu.roll(both[2 * p], 64, 1), both[2 * p + 1]) for p in range(2)]
    grads = [
        queries(query_all),
        jnp.concatenate(keys, axis=1).astype(jnp.bfloat16),
        jnp.concatenate(values, axis=1).astype(jnp.bfloat16),
    ]
    plain = jnp.zeros((ROWS, 1), jnp.float32)
    crossed = jnp.zeros((ROWS, 1), jnp.float32)
    for i in range(QUADS):
        span = slice(i * width, (i + 1) * width)
        part = sum(
            lax.dot_general(grads[k], w[k, span, :], NT, preferred_element_type=jnp.float32)
            for k in range(3)
        )
        grad_send[i] = part.astype(jnp.bfloat16)
        scaled = part * gain[:, span]
        plain = plain + jnp.sum(scaled, axis=1, keepdims=True)
        crossed = crossed + jnp.sum(scaled * unit[i], axis=1, keepdims=True)
    lane = lanes(ROWS)
    sums_send[...] = jnp.where(lane == 0, plain, jnp.where(lane == 1, crossed, 0.0)).T[0:8]
    scattered = []
    for h in heads:
        scattered.append(copies.to(grad_send.at[h], grad_recv.at[mine], {"head": h}))
        scattered.append(copies.to(sums_send, sums_recv.at[mine], {"head": h}))
    grad_recv[mine] = grad_send[mine]
    sums_recv[mine] = sums_send[...]

    received(outs_back)
    attended = queries(attended_all)
    for i in range(QUADS):
        span = slice(i * width, (i + 1) * width)
        branch_send[i] = jnp.dot(
            attended, w_out[:, span], preferred_element_type=jnp.float32
        ).astype(jnp.bfloat16)
    branches = [copies.to(branch_send.at[h], branch_recv.at[mine], {"head": h}) for h in heads]
    branch_recv[mine] = branch_send[mine]

    own_unit = jnp.zeros((ROWS, width), jnp.float32)
    own_gain = jnp.zeros((1, width), jnp.float32)
    for i in range(QUADS):
        own_unit = jnp.where(mine == i, unit[i], own_unit)
        own_gain = jnp.where(mine == i, gain[:, i * width : (i + 1) * width], own_gain)
    received(scattered)
    sums = (sums_recv[0] + sums_recv[1]) + (sums_recv[2] + sums_recv[3])
    means = jnp.concatenate([sums, jnp.zeros((120, 128), jnp.float32)], axis=0).T / (QUADS * width)
    scaled = total(grad_recv, range(QUADS)) * own_gain
    inner = scaled - means[:, 0:1] - own_unit * means[:, 1:2]
    upstream = grad[...].astype(jnp.float32) * column
    source[...] = ((upstream + inner * spread) * column).astype(jnp.bfloat16)
    halos = [
        copies.to(source.at[pl.ds(32, 96)], above, {"ctx": after}),
        copies.to(source.at[pl.ds(0, 96)], below, {"ctx": before}),
    ]

    received(branches)
    branch = total(branch_recv, range(QUADS))
    residual = full[mine].astype(jnp.float32)
    encoded[...] = ((residual + branch * keep * KEEP_SCALE) * column).astype(jnp.bfloat16)
    outs = [copies.here(encoded, encoded_out)]

    received(halos)
    for cols, part in depthwise(
        True, source[...], above[...], below[...], taps, None, alive, padded
    ):
        result[:, cols] = part.astype(jnp.bfloat16)
    outs.append(copies.here(result, tokens_out))
    for copy in outs:
        copy.wait()
    copies.sent()


def remote_call(body, collective_id, outs, scratch, far, near, *args):
    smem = pl.BlockSpec(memory_space=pltpu.SMEM)
    return pl.pallas_call(
        body,
        out_shape=outs,
        in_specs=[smem if a.shape == (2,) else ANY for a in args],
        out_specs=[ANY] * len(outs),
        scratch_shapes=scratch
        + [
            pltpu.SemaphoreType.DMA((far,)),
            pltpu.SemaphoreType.DMA((far,)),
            pltpu.SemaphoreType.DMA((near,)),
        ],
        compiler_params=pltpu.CompilerParams(
            collective_id=collective_id, has_side_effects=True, vmem_limit_bytes=WHOLE
        ),
    )(*args)


def on_device(tokens, tissue, conv_taps, conv_bias, ln_gain, w_qkv, w_out, drop_seed, grad_out):
    rows, width = tokens.shape
    gain_row = ln_gain[None, :]
    bias_row = conv_bias[None, :]
    tissue_row = tissue[None, :]
    weights_in = w_qkv.transpose(1, 0, 2)
    half, whole = (HALF, 128), (ROWS, 128)

    def held(shape, dtype=jnp.bfloat16):
        return pltpu.VMEM(shape, dtype)

    def like(array):
        return pltpu.VMEM(array.shape, array.dtype)

    padded = held((rows // GRID_COLS + 6, 48, width), jnp.float32)
    query_all, grad_all, key_all, full = remote_call(
        front_kernel,
        1,
        [
            struct((BLOCKS,) + half),
            struct((BLOCKS,) + half),
            struct((BLOCKS,) + whole),
            struct((QUADS, rows, width)),
        ],
        [
            like(tokens),
            like(tissue_row),
            like(grad_out),
            like(conv_taps),
            like(bias_row),
            like(gain_row),
            like(weights_in),
            like(w_out),
            held((rows, width)),
            held((96, width)),
            held((96, width)),
            held((QUADS, rows, width)),
            held((QUADS, rows, width)),
            held((QUADS,) + half),
            held((QUADS,) + half),
            held((QUADS,) + whole),
            padded,
        ],
        53,
        12,
        drop_seed,
        tokens,
        tissue_row,
        grad_out,
        conv_taps,
        bias_row,
        gain_row,
        weights_in,
        w_out,
    )
    weights, attended, stat = attention_forward(query_all, grad_all, key_all)
    (stats,) = remote_call(
        stat_kernel, 2, [struct((4, 32, 128), jnp.float32)], [], 3, 1, stat
    )
    out_part, query_part, key_part = attention_backward(
        query_all, grad_all, key_all, weights, attended, stat, stats
    )
    encoded, grad_tokens = remote_call(
        back_kernel,
        3,
        [struct((rows, width))] * 2,
        [
            like(tissue_row),
            like(grad_out),
            like(conv_taps),
            like(gain_row),
            like(weights_in),
            like(w_out),
            held((QUADS, rows, width)),
            held((BLOCKS,) + half),
            held((BLOCKS,) + half),
            held((BLOCKS,) + whole),
            held((QUADS, rows, width)),
            held((QUADS, rows, width)),
            held((QUADS, rows, width)),
            held((QUADS, rows, width)),
            held((8, rows), jnp.float32),
            held((QUADS, 8, rows), jnp.float32),
            held((rows, width)),
            held((96, width)),
            held((96, width)),
            held((rows, width)),
            held((rows, width)),
            padded,
        ],
        56,
        12,
        drop_seed,
        out_part,
        query_part,
        key_part,
        full,
        tissue_row,
        grad_out,
        conv_taps,
        gain_row,
        weights_in,
        w_out,
    )
    return (encoded, grad_tokens)


def solution(mesh):
    placed = (
        P("ctx", "head"),
        P("ctx"),
        P(None, "head"),
        P("head"),
        P(),
        P(None, None, "head"),
        P("head", None),
        P(),
        P("ctx", "head"),
    )
    return jax.shard_map(
        on_device,
        mesh=mesh,
        in_specs=placed,
        out_specs=(P("ctx", "head"), P("ctx", "head")),
        check_vma=False,
    )
```

```python
import jax
import jax.numpy as jnp
from jax import lax
from jax.experimental import pallas as pl
from jax.experimental.pallas import tpu as pltpu
from jax.sharding import PartitionSpec as P

HEAD_DIM = 64
GRID_COLS = 32
ROWS = 128
QUADS = 4
BLOCKS = 16
SPAN = BLOCKS * ROWS
CHUNK = 256
HALF = ROWS // 2
WHOLE = 60 << 20
WIDTHS = (512, 768, 1024, 1536, 2048)

DROP_LEVEL = 103
KEEP_SCALE = 1024.0 / 921.0
NEG = -1e30
EPS = 1e-05
DEAD = 2.0**100

MESH = pl.DeviceIdType.MESH
ANY = pl.BlockSpec(memory_space=pl.ANY)
NT = (((1,), (1,)), ((), ()))


def struct(shape, dtype=jnp.bfloat16):
    return jax.ShapeDtypeStruct(shape, dtype)


def div(a, b):
    return lax.div(a, jnp.int32(b))


def mod(a, b):
    return lax.rem(a, jnp.int32(b))


def place():
    ctx = lax.axis_index("ctx")
    return ctx, div(ctx, 16), mod(div(ctx, 8), 2), mod(ctx, 8)


def query_peers():
    ctx, x, y, z = place()
    mine = mod(ctx, 16)
    peers = []
    for step in range(1, 16):
        to = mod(mine + step, 16)
        peers.append((x * 16 + to, to, 2 * div(to, 8) + mod(to, 2)))
    return mine, 2 * y + mod(z, 2), peers


def key_peers():
    ctx, x, y, z = place()
    mine = x * 4 + y * 2 + mod(z, 2)
    base = 2 * div(z, 2)
    peers = []
    for step in range(1, 16):
        to = mod(mine + step, 16)
        peers.append((div(to, 2) * 8 + base + mod(to, 2), to, mod(to, 4)))
    return mine, 2 * y + mod(z, 2), peers


def stat_peers():
    ctx, x, y, z = place()
    mine = div(z, 2)
    base = ctx - z + mod(z, 2)
    peers = []
    for step in range(1, 4):
        to = mod(mine + step, 4)
        peers.append((base + to * 2, to))
    return mine, peers


def head_peers():
    mine = lax.axis_index("head")
    return mine, [mod(mine + step, 4) for step in range(1, 4)]


class Copies:
    def __init__(self, send, recv, own):
        self.send, self.recv, self.own = send, recv, own
        self.far, self.near = [], []

    def to(self, src, dst, device):
        at = len(self.far)
        copy = pltpu.make_async_remote_copy(
            src_ref=src,
            dst_ref=dst,
            send_sem=self.send.at[at],
            recv_sem=self.recv.at[at],
            device_id=device,
            device_id_type=MESH,
        )
        copy.start()
        self.far.append(copy)
        return copy

    def here(self, src, dst):
        copy = pltpu.make_async_copy(src, dst, self.own.at[len(self.near)])
        copy.start()
        self.near.append(copy)
        return copy

    def sent(self):
        for copy in self.far:
            copy.wait_send()


def received(copies):
    for copy in copies:
        copy.wait_recv()


def ring_ids():
    ctx = lax.axis_index("ctx")
    return mod(ctx + 63, 64), mod(ctx + 1, 64)


def everyone():
    before, after = ring_ids()
    ids = [{"ctx": before}, {"ctx": after}]
    ids += [{"head": h} for h in head_peers()[1]]
    ids += [{"ctx": c} for c, _, _ in query_peers()[2]]
    return ids + [{"ctx": c} for c, _, _ in key_peers()[2]]


def announce(ids):
    barrier = pltpu.get_barrier_semaphore()
    for device in ids:
        pl.semaphore_signal(barrier, inc=1, device_id=device, device_id_type=MESH)


def all_here(ids):
    pl.semaphore_wait(pltpu.get_barrier_semaphore(), len(ids))


def stat_kernel(stats, stats_all, send, recv, own):
    mine, peers = stat_peers()
    ids = [{"ctx": c} for c, _ in peers]
    announce(ids)
    copies = Copies(send, recv, own)
    kept = copies.here(stats, stats_all.at[mine])
    all_here(ids)
    for device in ids:
        copies.to(stats, stats_all.at[mine], device)
    kept.wait()
    received(copies.far)
    copies.sent()


def lanes(rows, width=128):
    return lax.broadcasted_iota(jnp.int32, (rows, width), 1)


def normalised(full_ref):
    parts = [full_ref[i].astype(jnp.float32) for i in range(QUADS)]
    width = QUADS * parts[0].shape[1]
    mean = sum(jnp.sum(p, axis=1, keepdims=True) for p in parts) / width
    parts = [p - mean for p in parts]
    var = sum(jnp.sum(p * p, axis=1, keepdims=True) for p in parts) / width
    spread = lax.rsqrt(var + EPS)
    return [p * spread for p in parts], spread


def fold(top, bottom, low_half):
    low = lanes(top.shape[0]) < HEAD_DIM
    if low_half:
        return jnp.where(low, top, pltpu.roll(bottom, 64, 1))
    return jnp.where(low, pltpu.roll(top, 64, 1), bottom)


def fold_rows(block, low_half):
    return fold(block[0:64], block[64:128], low_half)


def unfold_rows(packed, low_half):
    moved = pltpu.roll(packed, 64, 1)
    return jnp.concatenate([packed, moved] if low_half else [moved, packed], axis=0)


def query_block(q_ref, d_ref, at):
    q = unfold_rows(q_ref[at].astype(jnp.float32), False)
    d = unfold_rows(d_ref[at].astype(jnp.float32), True)
    alive = q[:, HEAD_DIM : HEAD_DIM + 1] < DEAD / 2
    return jnp.where(alive, jnp.where(lanes(ROWS) < HEAD_DIM, d, q), 0.0), alive


def extra_lanes(rows, alive):
    lane = lanes(rows)
    return jnp.where(lane == 0, jnp.where(alive, 0.0, NEG), jnp.where(lane < 4, 1.0, 0.0))


def key_block(vk_ref, at):
    part = vk_ref[at].astype(jnp.float32)
    alive = part[:, 0:1] < DEAD / 2
    return jnp.concatenate([jnp.where(alive, part, 0.0), extra_lanes(ROWS, alive)], axis=1), alive


def count(alive):
    return (jnp.sum(jnp.where(alive, 1.0, 0.0)).astype(jnp.int32) + 15) // 16 * 16


def rows_at(start, count_, multiple):
    return pl.ds(pl.multiple_of(start, multiple), count_)


def by_width(size, run):
    low = 0
    for width in WIDTHS:

        @pl.when((size > low) & (size <= width))
        def _(width=width):
            run(width)

        low = width


def scores_of(qd, keys):
    lane = lanes(CHUNK)
    left = jnp.concatenate(
        [jnp.where(lane >= HEAD_DIM, qd * 0.125, 0.0), jnp.where(lane == 0, 1.0, 0.0)], axis=1
    ).astype(jnp.bfloat16)
    return lax.dot_general(left, keys, NT, preferred_element_type=jnp.float32)


def forward_kernel(q_ref, d_ref, vk_ref, keys, qd, o_ref, stat_ref, starts):
    nothing = jnp.concatenate(
        [jnp.zeros((ROWS, 128), jnp.float32), extra_lanes(ROWS, False)], axis=1
    ).astype(jnp.bfloat16)
    for block in range(BLOCKS + 1):
        keys[block * ROWS : (block + 1) * ROWS, :] = nothing
    qd[...] = jnp.zeros_like(qd)
    o_ref[...] = jnp.zeros_like(o_ref)
    stat_ref[...] = jnp.zeros_like(stat_ref)
    key_end = jnp.int32(0)
    query_end = jnp.int32(0)
    for block in range(BLOCKS):
        part, alive = key_block(vk_ref, block)
        starts[block] = key_end
        keys[rows_at(key_end, ROWS, 16), :] = part.astype(jnp.bfloat16)
        key_end = key_end + count(alive)
        part, alive = query_block(q_ref, d_ref, block)
        starts[BLOCKS + block] = query_end
        qd[rows_at(query_end, ROWS, 16), :] = part.astype(jnp.bfloat16)
        query_end = query_end + count(alive)
    starts[2 * BLOCKS] = key_end
    starts[2 * BLOCKS + 1] = query_end
    lane = lanes(CHUNK)

    def run(width):
        def chunk(step, _):
            rows = rows_at(step * CHUNK, CHUNK, CHUNK)
            here = qd[rows, :].astype(jnp.float32)
            scores = scores_of(here, keys[0:width, :])
            highest = jnp.max(scores, axis=1, keepdims=True)
            weights = jnp.exp(scores - highest).astype(jnp.bfloat16)
            summed = jnp.dot(weights, keys[0:width, :], preferred_element_type=jnp.float32)
            totals = summed[:, 129:130]
            attended = summed[:, 0:128] / totals
            o_ref[rows, :] = attended
            inner = jnp.sum(
                jnp.where(lane < HEAD_DIM, attended * here, 0.0), axis=1, keepdims=True
            )
            log_total = highest + jnp.log(totals)
            table = jnp.where(lane == 0, log_total, jnp.where(lane == 1, inner, 0.0)).T
            for kind in range(2):
                for half in range(2):
                    stat_ref[pl.ds(16 * kind + 2 * step + half, 1), :] = table[
                        kind : kind + 1, half * 128 : half * 128 + 128
                    ]
            return 0

        lax.fori_loop(0, (query_end + CHUNK - 1) // CHUNK, chunk, 0)

    by_width(key_end, run)


def backward_kernel(
    starts,
    keys,
    qd_ref,
    o_ref,
    stat_ref,
    stats_ref,
    out_ref,
    query_ref,
    grad_ref,
    table,
    query_acc,
    value_acc,
    key_acc,
    key_rows,
):
    logs = [stats_ref[i, 0:16, :] for i in range(4)]
    top = jnp.maximum(jnp.maximum(logs[0], logs[1]), jnp.maximum(logs[2], logs[3]))
    total = top + jnp.log(sum(jnp.exp(part - top) for part in logs))
    shift = sum(jnp.exp(logs[i] - total) * stats_ref[i, 16:32, :] for i in range(4))
    share = jnp.exp(stat_ref[0:16, :] - total)
    table[...] = jnp.concatenate(
        [share, shift, total, jnp.zeros((80, 128), jnp.float32)], axis=0
    ).T
    query_acc[...] = jnp.zeros_like(query_acc)
    key_rows[...] = jnp.zeros_like(key_rows)

    def column(kind, block):
        here = jnp.where(lanes(ROWS) == 16 * kind + block, table[...], 0.0)
        return jnp.sum(here, axis=1, keepdims=True)

    def columns(kind, step):
        return jnp.concatenate([column(kind, 2 * step), column(kind, 2 * step + 1)], axis=0)

    lane = lanes(CHUNK)

    def run(width):
        value_acc[:, 0:width] = jnp.zeros((HEAD_DIM, width), jnp.float32)
        key_acc[:, 0:width] = jnp.zeros((HEAD_DIM, width), jnp.float32)

        def chunk(step, _):
            rows = rows_at(step * CHUNK, CHUNK, CHUNK)
            qd = qd_ref[rows, :].astype(jnp.float32)
            shift, total = columns(1, step), columns(2, step)
            probs = jnp.exp(scores_of(qd, keys[0:width, :]) - total)
            high = shift.astype(jnp.bfloat16).astype(jnp.float32)
            middle = (shift - high).astype(jnp.bfloat16).astype(jnp.float32)
            low = shift - high - middle
            extra = jnp.where(
                lane == 1, -high, jnp.where(lane == 2, -middle, jnp.where(lane == 3, -low, 0.0))
            )
            left = jnp.concatenate([jnp.where(lane < HEAD_DIM, qd, 0.0), extra], axis=1)
            dprob = lax.dot_general(
                left.astype(jnp.bfloat16), keys[0:width, :], NT, preferred_element_type=jnp.float32
            )
            slope = (probs * dprob).astype(jnp.bfloat16)
            query_acc[rows, :] = (
                jnp.dot(slope, keys[0:width, 0:128], preferred_element_type=jnp.float32) * 0.125
            )
            scaled = (qd * jnp.where(lane < HEAD_DIM, 1.0, 0.125)).T.astype(jnp.bfloat16)
            value_acc[:, 0:width] += jnp.dot(
                scaled[0:64], probs.astype(jnp.bfloat16), preferred_element_type=jnp.float32
            )
            key_acc[:, 0:width] += jnp.dot(
                scaled[64:128], slope, preferred_element_type=jnp.float32
            )
            return 0

        lax.fori_loop(0, (starts[2 * BLOCKS + 1] + CHUNK - 1) // CHUNK, chunk, 0)
        for at in range(0, width, ROWS):
            both = jnp.concatenate(
                [value_acc[:, at : at + ROWS], key_acc[:, at : at + ROWS]], axis=0
            )
            key_rows[at : at + ROWS, :] = both.T.astype(jnp.bfloat16)

    by_width(starts[2 * BLOCKS], run)
    for block in range(BLOCKS):
        rows = rows_at(starts[block], ROWS, 16)
        grad_ref[block] = key_rows[rows, :]
        rows = rows_at(starts[BLOCKS + block], ROWS, 16)
        query_ref[block] = fold_rows(query_acc[rows, :], False).astype(jnp.bfloat16)

    for step in range(BLOCKS):
        rows = slice(step * ROWS, (step + 1) * ROWS)
        query_acc[rows, :] = o_ref[rows, :] * column(0, step)
    for block in range(BLOCKS):
        rows = rows_at(starts[BLOCKS + block], ROWS, 16)
        out_ref[block] = fold_rows(query_acc[rows, :], True).astype(jnp.bfloat16)


def whole(shape):
    return pl.BlockSpec(shape, lambda i: (0,) * len(shape))


def attention_forward(query_all, grad_all, key_all):
    room = SPAN + ROWS
    outs = [
        struct((room, 256)),
        struct((room, 128)),
        struct((room, 128), jnp.float32),
        struct((32, 128), jnp.float32),
    ]
    return pl.pallas_call(
        forward_kernel,
        grid=(1,),
        in_specs=[whole(a.shape) for a in (query_all, grad_all, key_all)],
        out_specs=[whole(out.shape) for out in outs] + [pl.BlockSpec(memory_space=pltpu.SMEM)],
        out_shape=outs + [struct((2 * BLOCKS + 2,), jnp.int32)],
        compiler_params=pltpu.CompilerParams(vmem_limit_bytes=WHOLE),
    )(query_all, grad_all, key_all)


def attention_backward(starts, keys, qd, attended, stat, stats):
    room = SPAN + ROWS
    half = struct((BLOCKS, HALF, 128))
    outs = [half, half, struct((BLOCKS, ROWS, 128))]
    return pl.pallas_call(
        backward_kernel,
        grid=(1,),
        in_specs=[pl.BlockSpec(memory_space=pltpu.SMEM)]
        + [whole(a.shape) for a in (keys, qd, attended, stat, stats)],
        out_specs=[whole(out.shape) for out in outs],
        out_shape=outs,
        scratch_shapes=[
            pltpu.VMEM((128, 128), jnp.float32),
            pltpu.VMEM((room, 128), jnp.float32),
            pltpu.VMEM((HEAD_DIM, SPAN), jnp.float32),
            pltpu.VMEM((HEAD_DIM, SPAN), jnp.float32),
            pltpu.VMEM((room, 128), jnp.bfloat16),
        ],
        compiler_params=pltpu.CompilerParams(vmem_limit_bytes=WHOLE),
    )(starts, keys, qd, attended, stat, stats)


def keep_mask(anchor, counter, row_ids, col_ids):
    mixed = (
        row_ids * jnp.int32(374761393)
        + col_ids * jnp.int32(668265263)
        + anchor * jnp.int32(1274126177)
        + counter
    )
    mixed = jnp.bitwise_xor(mixed, lax.shift_right_logical(mixed, jnp.full_like(mixed, 15)))
    mixed = mixed * jnp.int32(16777619)
    mixed = jnp.bitwise_xor(mixed, lax.shift_right_logical(mixed, jnp.full_like(mixed, 13)))
    mixed = mixed * jnp.int32(1274126177)
    mixed = jnp.bitwise_xor(mixed, lax.shift_right_logical(mixed, jnp.full_like(mixed, 16)))
    return (jnp.bitwise_and(mixed, jnp.int32(1023)) >= DROP_LEVEL).astype(jnp.float32)


def own_keep(seed_ref, rows, width):
    row_ids = lax.axis_index("ctx") * rows + lax.broadcasted_iota(jnp.int32, (rows, width), 0)
    col_ids = lax.axis_index("head") * width + lax.broadcasted_iota(jnp.int32, (rows, width), 1)
    return keep_mask(seed_ref[0], seed_ref[1], row_ids, col_ids)


def compaction(tissue_ref):
    row = tissue_ref[...].astype(jnp.float32)
    up = lax.broadcasted_iota(jnp.int32, (ROWS, ROWS), 0)
    over = lax.broadcasted_iota(jnp.int32, (ROWS, ROWS), 1)
    upper = jnp.where(up <= over, 1.0, 0.0).astype(jnp.bfloat16)
    wide = jnp.broadcast_to(row, (16, ROWS)).astype(jnp.bfloat16)
    rank = jnp.dot(wide, upper, preferred_element_type=jnp.float32)[0:1]
    at = up.astype(jnp.float32)
    pack = jnp.where((at == rank - 1.0) & (row > 0.0), 1.0, 0.0)
    return pack, at >= jnp.sum(row, axis=1, keepdims=True)


def moved_rows(pack, rows):
    return jnp.dot(
        pack.astype(jnp.bfloat16), rows.astype(jnp.bfloat16), preferred_element_type=jnp.float32
    )


def alive_column(tissue_ref):
    row = tissue_ref[...].astype(jnp.float32)
    return jnp.broadcast_to(row, (ROWS, ROWS)).T


def merged_tap(taps_ref, row, col, cols):
    tap = taps_ref[row * 7 + col : row * 7 + col + 1, cols]
    if 1 <= row <= 5 and 1 <= col <= 5:
        at = 49 + (row - 1) * 5 + col - 1
        tap = tap + taps_ref[at : at + 1, cols]
    if 2 <= row <= 4 and 2 <= col <= 4:
        at = 74 + (row - 2) * 3 + col - 2
        tap = tap + taps_ref[at : at + 1, cols]
    return tap


def depthwise(flipped, field, above, below, taps_ref, bias, padded):
    ctx = lax.axis_index("ctx")
    width = field.shape[1]
    grid_rows = ROWS // GRID_COLS
    has_above = jnp.where(ctx > 0, 1.0, 0.0)
    has_below = jnp.where(ctx < 63, 1.0, 0.0)
    field = field.astype(jnp.float32)
    padded[:, 0:8, :] = jnp.zeros((grid_rows + 6, 8, width), jnp.float32)
    padded[:, 40:48, :] = jnp.zeros((grid_rows + 6, 8, width), jnp.float32)
    padded[0:3, 8:40, :] = (above.astype(jnp.float32) * has_above).reshape(3, GRID_COLS, width)
    padded[3:7, 8:40, :] = field.reshape(grid_rows, GRID_COLS, width)
    padded[7:10, 8:40, :] = (below.astype(jnp.float32) * has_below).reshape(3, GRID_COLS, width)
    for start in range(0, width, 128):
        cols = slice(start, start + 128)
        total = field[:, cols].reshape(grid_rows, GRID_COLS, 128)
        if bias is not None:
            total = total + bias[:, cols].reshape(1, 1, 128)
        for col in range(7):
            moved = padded[:, 5 + col : 37 + col, cols]
            for row in range(7):
                if flipped:
                    tap = merged_tap(taps_ref, 6 - row, 6 - col, cols)
                else:
                    tap = merged_tap(taps_ref, row, col, cols)
                total = total + tap.reshape(1, 1, 128) * moved[row : row + grid_rows]
        yield cols, total.reshape(ROWS, 128)


def front_kernel(
    seed_ref,
    tokens_in,
    tissue_in,
    grad_in,
    taps_in,
    bias_in,
    gain_in,
    w_in,
    w_out_in,
    query_all,
    grad_all,
    key_all,
    full_all,
    tokens,
    tissue,
    grad,
    taps,
    bias,
    gain,
    w,
    w_out,
    masked,
    above,
    below,
    drop_full,
    full,
    query_part,
    grad_part,
    key_part,
    padded,
    send,
    recv,
    own,
):
    rows, width = tokens.shape
    ids = everyone()
    announce(ids)
    copies = Copies(send, recv, own)
    first = [
        copies.here(src, dst)
        for src, dst in ((tokens_in, tokens), (tissue_in, tissue), (grad_in, grad))
    ]
    for_conv = [copies.here(taps_in, taps), copies.here(bias_in, bias)]
    for_grad = [copies.here(w_out_in, w_out)]
    for_project = [copies.here(gain_in, gain), copies.here(w_in, w)]
    before, after = ring_ids()
    mine, heads = head_peers()
    keep = own_keep(seed_ref, rows, width)
    for copy in first:
        copy.wait()
    alive = alive_column(tissue)
    column = alive[:, 0:1]
    masked[...] = (tokens[...].astype(jnp.float32) * column).astype(jnp.bfloat16)
    all_here(ids)
    halos = [
        copies.to(masked.at[pl.ds(32, 96)], above, {"ctx": after}),
        copies.to(masked.at[pl.ds(0, 96)], below, {"ctx": before}),
    ]
    upstream = grad[...].astype(jnp.float32) * column
    drop_full[mine] = (upstream * keep * KEEP_SCALE).astype(jnp.bfloat16)
    drops = [copies.to(drop_full.at[mine], drop_full.at[mine], {"head": h}) for h in heads]

    q_mine, slot, q_peers = query_peers()
    k_mine, _, k_peers = key_peers()
    for copy in for_grad:
        copy.wait()
    received(drops)
    out_grad = sum(
        lax.dot_general(
            drop_full[i],
            w_out[:, i * width : (i + 1) * width],
            NT,
            preferred_element_type=jnp.float32,
        )
        for i in range(QUADS)
    )
    pack, dead = compaction(tissue)
    out_grad = moved_rows(pack, out_grad)
    for j in range(QUADS):
        pair = out_grad[:, 128 * (j // 2) : 128 * (j // 2) + 128]
        grad_part[j] = fold_rows(pair, j % 2 == 0).astype(jnp.bfloat16)
    landing = [
        copies.to(grad_part.at[h], grad_all.at[q_mine], {"ctx": c}) for c, _, h in q_peers
    ]
    local = [copies.here(grad_part.at[slot], grad_all.at[q_mine])]

    for copy in for_conv:
        copy.wait()
    received(halos)
    for cols, part in depthwise(
        False, masked[...], above[...], below[...], taps, bias[...].reshape(1, width), padded
    ):
        full[mine, :, cols] = (part * alive).astype(jnp.bfloat16)
    parts = [copies.to(full.at[mine], full.at[mine], {"head": h}) for h in heads]

    for copy in for_project:
        copy.wait()
    received(parts)
    local.append(copies.here(full, full_all))
    unit, _ = normalised(full)
    gain_row = gain[...].reshape(1, QUADS * width)
    sums = [jnp.zeros((rows, w.shape[2]), jnp.float32) for _ in range(3)]
    for i in range(QUADS):
        span = slice(i * width, (i + 1) * width)
        normed = (unit[i] * gain_row[:, span]).astype(jnp.bfloat16)
        for k in range(3):
            sums[k] = sums[k] + jnp.dot(normed, w[k, span, :], preferred_element_type=jnp.float32)
    low = lanes(ROWS) < HEAD_DIM
    sums = [moved_rows(pack, part) for part in sums]
    for j in range(QUADS):
        q, k, v = (part[:, 128 * (j // 2) : 128 * (j // 2) + 128] for part in sums)
        q = jnp.where(dead, DEAD, q)
        query_part[j] = fold_rows(q, j % 2 == 0).astype(jnp.bfloat16)
        if j % 2 == 0:
            both = jnp.where(low, v, pltpu.roll(k, 64, 1))
        else:
            both = jnp.where(low, pltpu.roll(v, 64, 1), k)
        key_part[j] = jnp.where(dead, DEAD, both).astype(jnp.bfloat16)
    for (qc, _, qh), (kc, _, kh) in zip(q_peers, k_peers):
        landing.append(copies.to(key_part.at[kh], key_all.at[k_mine], {"ctx": kc}))
        landing.append(copies.to(query_part.at[qh], query_all.at[q_mine], {"ctx": qc}))
    local.append(copies.here(query_part.at[slot], query_all.at[q_mine]))
    local.append(copies.here(key_part.at[slot], key_all.at[k_mine]))
    for copy in local:
        copy.wait()
    received(landing)
    copies.sent()


def back_kernel(
    seed_ref,
    attended_in,
    query_in,
    key_in,
    full_in,
    tissue_in,
    grad_in,
    taps_in,
    gain_in,
    w_in,
    w_out_in,
    encoded_out,
    tokens_out,
    tissue,
    grad,
    taps,
    gain,
    w,
    w_out,
    full,
    attended_all,
    query_all,
    key_all,
    grad_send,
    grad_recv,
    branch_send,
    branch_recv,
    sums_send,
    sums_recv,
    source,
    above,
    below,
    encoded,
    result,
    padded,
    send,
    recv,
    own,
):
    rows, width = grad.shape
    ids = everyone()
    announce(ids)
    copies = Copies(send, recv, own)
    q_mine, _, q_peers = query_peers()
    k_mine, _, k_peers = key_peers()
    first = [
        copies.here(src, dst)
        for src, dst in ((tissue_in, tissue), (grad_in, grad), (full_in, full), (gain_in, gain))
    ]
    later = [copies.here(src, dst) for src, dst in ((w_in, w), (w_out_in, w_out), (taps_in, taps))]
    kept = [
        copies.here(query_in.at[q_mine], query_all.at[q_mine]),
        copies.here(key_in.at[k_mine], key_all.at[k_mine]),
        copies.here(attended_in.at[q_mine], attended_all.at[q_mine]),
    ]
    all_here(ids)
    grads_back, outs_back = [], []
    for (qc, qd, _), (kc, kd, _) in zip(q_peers, k_peers):
        grads_back.append(copies.to(key_in.at[kd], key_all.at[k_mine], {"ctx": kc}))
        grads_back.append(copies.to(query_in.at[qd], query_all.at[q_mine], {"ctx": qc}))
    for qc, qd, _ in q_peers:
        outs_back.append(copies.to(attended_in.at[qd], attended_all.at[q_mine], {"ctx": qc}))

    mine, heads = head_peers()
    before, after = ring_ids()
    for copy in first + later:
        copy.wait()
    keep = own_keep(seed_ref, rows, width)
    alive = alive_column(tissue)
    column = alive[:, 0:1]
    unit, spread = normalised(full)
    gain_row = gain[...].reshape(1, QUADS * width)
    low = lanes(ROWS) < HEAD_DIM
    unpack = compaction(tissue)[0].T

    def total(ref, slots):
        parts = [ref[s].astype(jnp.float32) for s in slots]
        return (parts[0] + parts[1]) + (parts[2] + parts[3])

    def queries(ref):
        heads_ = []
        for j in range(QUADS):
            packed = total(ref, [8 * (j // 2) + 2 * k + j % 2 for k in range(4)])
            heads_.append(unfold_rows(packed, j % 2 == 0))
        pairs = [jnp.where(low, heads_[2 * p], heads_[2 * p + 1]) for p in range(2)]
        return moved_rows(unpack, jnp.concatenate(pairs, axis=1)).astype(jnp.bfloat16)

    for copy in kept:
        copy.wait()
    received(grads_back)
    both = [total(key_all, [4 * k + j for k in range(4)]) for j in range(QUADS)]
    values = [jnp.where(low, both[2 * p], pltpu.roll(both[2 * p + 1], 64, 1)) for p in range(2)]
    keys = [jnp.where(low, pltpu.roll(both[2 * p], 64, 1), both[2 * p + 1]) for p in range(2)]
    grads = [
        queries(query_all),
        moved_rows(unpack, jnp.concatenate(keys, axis=1)).astype(jnp.bfloat16),
        moved_rows(unpack, jnp.concatenate(values, axis=1)).astype(jnp.bfloat16),
    ]
    plain = jnp.zeros((ROWS, 1), jnp.float32)
    crossed = jnp.zeros((ROWS, 1), jnp.float32)
    for i in range(QUADS):
        span = slice(i * width, (i + 1) * width)
        part = sum(
            lax.dot_general(grads[k], w[k, span, :], NT, preferred_element_type=jnp.float32)
            for k in range(3)
        )
        grad_send[i] = part.astype(jnp.bfloat16)
        scaled = part * gain_row[:, span]
        plain = plain + jnp.sum(scaled, axis=1, keepdims=True)
        crossed = crossed + jnp.sum(scaled * unit[i], axis=1, keepdims=True)
    lane = lanes(ROWS)
    sums_send[...] = jnp.where(lane == 0, plain, jnp.where(lane == 1, crossed, 0.0)).T[0:8]
    scattered = []
    for h in heads:
        scattered.append(copies.to(grad_send.at[h], grad_recv.at[mine], {"head": h}))
        scattered.append(copies.to(sums_send, sums_recv.at[mine], {"head": h}))
    grad_recv[mine] = grad_send[mine]
    sums_recv[mine] = sums_send[...]

    received(outs_back)
    attended = queries(attended_all)
    for i in range(QUADS):
        span = slice(i * width, (i + 1) * width)
        branch_send[i] = jnp.dot(
            attended, w_out[:, span], preferred_element_type=jnp.float32
        ).astype(jnp.bfloat16)
    branches = [copies.to(branch_send.at[h], branch_recv.at[mine], {"head": h}) for h in heads]
    branch_recv[mine] = branch_send[mine]

    own_unit = jnp.zeros((ROWS, width), jnp.float32)
    own_gain = jnp.zeros((1, width), jnp.float32)
    for i in range(QUADS):
        own_unit = jnp.where(mine == i, unit[i], own_unit)
        own_gain = jnp.where(mine == i, gain_row[:, i * width : (i + 1) * width], own_gain)
    received(scattered)
    sums = (sums_recv[0] + sums_recv[1]) + (sums_recv[2] + sums_recv[3])
    means = jnp.concatenate([sums, jnp.zeros((120, 128), jnp.float32)], axis=0).T / (QUADS * width)
    scaled = total(grad_recv, range(QUADS)) * own_gain
    inner = scaled - means[:, 0:1] - own_unit * means[:, 1:2]
    upstream = grad[...].astype(jnp.float32) * column
    source[...] = ((upstream + inner * spread) * column).astype(jnp.bfloat16)
    halos = [
        copies.to(source.at[pl.ds(32, 96)], above, {"ctx": after}),
        copies.to(source.at[pl.ds(0, 96)], below, {"ctx": before}),
    ]

    received(branches)
    branch = total(branch_recv, range(QUADS))
    residual = full[mine].astype(jnp.float32)
    encoded[...] = (residual + branch * keep * KEEP_SCALE).astype(jnp.bfloat16)
    outs = [copies.here(encoded, encoded_out)]

    received(halos)
    for cols, part in depthwise(
        True, source[...], above[...], below[...], taps, None, padded
    ):
        result[:, cols] = part.astype(jnp.bfloat16)
    outs.append(copies.here(result, tokens_out))
    for copy in outs:
        copy.wait()
    copies.sent()


def remote_call(body, collective_id, outs, scratch, far, near, *args):
    smem = pl.BlockSpec(memory_space=pltpu.SMEM)
    return pl.pallas_call(
        body,
        out_shape=outs,
        in_specs=[smem if a.shape == (2,) else ANY for a in args],
        out_specs=[ANY] * len(outs),
        scratch_shapes=scratch
        + [
            pltpu.SemaphoreType.DMA((far,)),
            pltpu.SemaphoreType.DMA((far,)),
            pltpu.SemaphoreType.DMA((near,)),
        ],
        compiler_params=pltpu.CompilerParams(
            collective_id=collective_id, has_side_effects=True, vmem_limit_bytes=WHOLE
        ),
    )(*args)


def on_device(tokens, tissue, conv_taps, conv_bias, ln_gain, w_qkv, w_out, drop_seed, grad_out):
    rows, width = tokens.shape
    tissue_row = tissue[None, :]
    weights_in = w_qkv.transpose(1, 0, 2)
    half, whole = (HALF, 128), (ROWS, 128)

    def held(shape, dtype=jnp.bfloat16):
        return pltpu.VMEM(shape, dtype)

    def like(array):
        return pltpu.VMEM(array.shape, array.dtype)

    padded = held((rows // GRID_COLS + 6, 48, width), jnp.float32)
    query_all, grad_all, key_all, full = remote_call(
        front_kernel,
        1,
        [
            struct((BLOCKS,) + half),
            struct((BLOCKS,) + half),
            struct((BLOCKS,) + whole),
            struct((QUADS, rows, width)),
        ],
        [
            like(tokens),
            like(tissue_row),
            like(grad_out),
            like(conv_taps),
            like(conv_bias),
            like(ln_gain),
            like(weights_in),
            like(w_out),
            held((rows, width)),
            held((96, width)),
            held((96, width)),
            held((QUADS, rows, width)),
            held((QUADS, rows, width)),
            held((QUADS,) + half),
            held((QUADS,) + half),
            held((QUADS,) + whole),
            padded,
        ],
        53,
        12,
        drop_seed,
        tokens,
        tissue_row,
        grad_out,
        conv_taps,
        conv_bias,
        ln_gain,
        weights_in,
        w_out,
    )
    keys, qd, attended, stat, starts = attention_forward(query_all, grad_all, key_all)
    (stats,) = remote_call(
        stat_kernel, 2, [struct((4, 32, 128), jnp.float32)], [], 3, 1, stat
    )
    out_part, query_part, key_part = attention_backward(
        starts, keys, qd, attended, stat, stats
    )
    encoded, grad_tokens = remote_call(
        back_kernel,
        3,
        [struct((rows, width))] * 2,
        [
            like(tissue_row),
            like(grad_out),
            like(conv_taps),
            like(ln_gain),
            like(weights_in),
            like(w_out),
            held((QUADS, rows, width)),
            held((BLOCKS,) + half),
            held((BLOCKS,) + half),
            held((BLOCKS,) + whole),
            held((QUADS, rows, width)),
            held((QUADS, rows, width)),
            held((QUADS, rows, width)),
            held((QUADS, rows, width)),
            held((8, rows), jnp.float32),
            held((QUADS, 8, rows), jnp.float32),
            held((rows, width)),
            held((96, width)),
            held((96, width)),
            held((rows, width)),
            held((rows, width)),
            padded,
        ],
        56,
        12,
        drop_seed,
        out_part,
        query_part,
        key_part,
        full,
        tissue_row,
        grad_out,
        conv_taps,
        ln_gain,
        weights_in,
        w_out,
    )
    alive = tissue.astype(jnp.bfloat16)[:, None]
    return (encoded * alive, grad_tokens * alive)


def solution(mesh):
    placed = (
        P("ctx", "head"),
        P("ctx"),
        P(None, "head"),
        P("head"),
        P(),
        P(None, None, "head"),
        P("head", None),
        P(),
        P("ctx", "head"),
    )
    return jax.shard_map(
        on_device,
        mesh=mesh,
        in_specs=placed,
        out_specs=(P("ctx", "head"), P("ctx", "head")),
        check_vma=False,
    )
```

```python
import jax
import jax.numpy as jnp
from jax import lax
from jax.experimental import pallas as pl
from jax.experimental.pallas import tpu as pltpu
from jax.sharding import PartitionSpec as P

HEAD_DIM = 64
GRID_COLS = 32
ROWS = 128
QUADS = 4
BLOCKS = 16
SPAN = BLOCKS * ROWS
CHUNK = 256
HALF = ROWS // 2
WHOLE = 60 << 20
CHUNKS = SPAN // CHUNK

DROP_LEVEL = 103
KEEP_SCALE = 1024.0 / 921.0
NEG = -1e30
EPS = 1e-05
DEAD = 2.0**100

MESH = pl.DeviceIdType.MESH
ANY = pl.BlockSpec(memory_space=pl.ANY)
NT = (((1,), (1,)), ((), ()))


def struct(shape, dtype=jnp.bfloat16):
    return jax.ShapeDtypeStruct(shape, dtype)


def div(a, b):
    return lax.div(a, jnp.int32(b))


def mod(a, b):
    return lax.rem(a, jnp.int32(b))


def place():
    ctx = lax.axis_index("ctx")
    return ctx, div(ctx, 16), mod(div(ctx, 8), 2), mod(ctx, 8)


def query_peers():
    ctx, x, y, z = place()
    mine = mod(ctx, 16)
    peers = []
    for step in range(1, 16):
        to = mod(mine + step, 16)
        peers.append((x * 16 + to, to, 2 * div(to, 8) + mod(to, 2)))
    return mine, 2 * y + mod(z, 2), peers


def key_peers():
    ctx, x, y, z = place()
    mine = x * 4 + y * 2 + mod(z, 2)
    base = 2 * div(z, 2)
    peers = []
    for step in range(1, 16):
        to = mod(mine + step, 16)
        peers.append((div(to, 2) * 8 + base + mod(to, 2), to, mod(to, 4)))
    return mine, 2 * y + mod(z, 2), peers


def stat_peers():
    ctx, x, y, z = place()
    mine = div(z, 2)
    base = ctx - z + mod(z, 2)
    peers = []
    for step in range(1, 4):
        to = mod(mine + step, 4)
        peers.append((base + to * 2, to))
    return mine, peers


def head_peers():
    mine = lax.axis_index("head")
    return mine, [mod(mine + step, 4) for step in range(1, 4)]


class Copies:
    def __init__(self, send, recv, own):
        self.send, self.recv, self.own = send, recv, own
        self.far, self.near = [], []

    def to(self, src, dst, device, recv=None):
        at = len(self.far)
        copy = pltpu.make_async_remote_copy(
            src_ref=src,
            dst_ref=dst,
            send_sem=self.send.at[at],
            recv_sem=self.recv.at[at] if recv is None else recv,
            device_id=device,
            device_id_type=MESH,
        )
        copy.start()
        self.far.append(copy)
        return copy

    def here(self, src, dst):
        copy = pltpu.make_async_copy(src, dst, self.own.at[len(self.near)])
        copy.start()
        self.near.append(copy)
        return copy

    def sent(self):
        for copy in self.far:
            copy.wait_send()


def received(copies):
    for copy in copies:
        copy.wait_recv()


def arriving(slot, send, recv, device):
    return pltpu.make_async_remote_copy(
        src_ref=slot,
        dst_ref=slot,
        send_sem=send,
        recv_sem=recv,
        device_id=device,
        device_id_type=MESH,
    )


def ring_ids():
    ctx = lax.axis_index("ctx")
    return mod(ctx + 63, 64), mod(ctx + 1, 64)


def everyone():
    before, after = ring_ids()
    ids = [{"ctx": before}, {"ctx": after}]
    ids += [{"head": h} for h in head_peers()[1]]
    ids += [{"ctx": c} for c, _, _ in query_peers()[2]]
    return ids + [{"ctx": c} for c, _, _ in key_peers()[2]]


def announce(ids):
    barrier = pltpu.get_barrier_semaphore()
    for device in ids:
        pl.semaphore_signal(barrier, inc=1, device_id=device, device_id_type=MESH)


def all_here(ids):
    pl.semaphore_wait(pltpu.get_barrier_semaphore(), len(ids))


def lanes(rows, width=128):
    return lax.broadcasted_iota(jnp.int32, (rows, width), 1)


def normalised(full_ref):
    parts = [full_ref[i].astype(jnp.float32) for i in range(QUADS)]
    width = QUADS * parts[0].shape[1]
    mean = sum(jnp.sum(p, axis=1, keepdims=True) for p in parts) / width
    parts = [p - mean for p in parts]
    var = sum(jnp.sum(p * p, axis=1, keepdims=True) for p in parts) / width
    spread = lax.rsqrt(var + EPS)
    return [p * spread for p in parts], spread


def fold(top, bottom, low_half):
    low = lanes(top.shape[0]) < HEAD_DIM
    if low_half:
        return jnp.where(low, top, pltpu.roll(bottom, 64, 1))
    return jnp.where(low, pltpu.roll(top, 64, 1), bottom)


def fold_rows(block, low_half):
    return fold(block[0:64], block[64:128], low_half)


def unfold_rows(packed, low_half):
    moved = pltpu.roll(packed, 64, 1)
    return jnp.concatenate([packed, moved] if low_half else [moved, packed], axis=0)


def query_chunk(q_ref, d_ref, at):
    blocks = []
    for block in range(CHUNK // ROWS):
        q = unfold_rows(q_ref[2 * at + block].astype(jnp.float32), False)
        d = unfold_rows(d_ref[2 * at + block].astype(jnp.float32), True)
        blocks.append(jnp.where(lanes(ROWS) < HEAD_DIM, d, q))
    return jnp.concatenate(blocks, axis=0)


def key_block(part):
    part = part.astype(jnp.float32)
    alive = part[:, 0:1] < DEAD / 2
    lane = lanes(ROWS)
    extra = jnp.where(lane == 0, jnp.where(alive, 0.0, NEG), jnp.where(lane < 4, 1.0, 0.0))
    return jnp.concatenate([jnp.where(alive, part, 0.0), extra], axis=1).astype(jnp.bfloat16)


def rows_at(start, count_, multiple):
    return pl.ds(pl.multiple_of(start, multiple), count_)


def scores_of(qd, keys):
    lane = lanes(CHUNK)
    left = jnp.concatenate(
        [jnp.where(lane >= HEAD_DIM, qd * 0.125, 0.0), jnp.where(lane == 0, 1.0, 0.0)], axis=1
    ).astype(jnp.bfloat16)
    return lax.dot_general(left, keys, NT, preferred_element_type=jnp.float32)


def forward_chunk(qd, keys, weights, rows, attended):
    lane = lanes(CHUNK)
    scores = scores_of(qd, keys[...])
    highest = jnp.max(scores, axis=1, keepdims=True)
    part = jnp.exp(scores - highest).astype(jnp.bfloat16)
    weights[rows, :] = part
    summed = jnp.dot(part, keys[...], preferred_element_type=jnp.float32)
    totals = summed[:, 129:130]
    mine = summed[:, 0:128] / totals
    attended[rows, :] = mine
    inner = jnp.sum(jnp.where(lane < HEAD_DIM, mine * qd, 0.0), axis=1, keepdims=True)
    log_total = highest + jnp.log(totals)
    table = jnp.where(
        lane == 0, log_total, jnp.where(lane == 1, inner, jnp.where(lane == 2, highest, 0.0))
    ).T
    parts = [table[k : k + 1, h : h + 128] for k in range(3) for h in (0, 128)]
    return jnp.concatenate(parts + [jnp.zeros((2, 128), jnp.float32)], axis=0)


def chunk_columns(stats, mine):
    logs = [stats[i][0:2] for i in range(4)]
    top = jnp.maximum(jnp.maximum(logs[0], logs[1]), jnp.maximum(logs[2], logs[3]))
    total = top + jnp.log(sum(jnp.exp(part - top) for part in logs))
    shift = sum(jnp.exp(logs[i] - total) * stats[i][2:4] for i in range(4))
    share = jnp.exp(mine[0:2] - total)
    factor = jnp.exp(mine[4:6] - total)
    rows = jnp.concatenate([share, shift, factor, jnp.zeros((122, 128), jnp.float32)], axis=0).T
    return [
        jnp.concatenate([rows[:, k : k + 1], rows[:, k + 1 : k + 2]], axis=0) for k in (0, 2, 4)
    ]


def backward_chunk(qd, keys, weights, shift, factor, value_acc, key_acc):
    lane = lanes(CHUNK)
    high = shift.astype(jnp.bfloat16).astype(jnp.float32)
    middle = (shift - high).astype(jnp.bfloat16).astype(jnp.float32)
    low = shift - high - middle
    extra = jnp.where(
        lane == 1, -high, jnp.where(lane == 2, -middle, jnp.where(lane == 3, -low, 0.0))
    )
    left = jnp.concatenate([jnp.where(lane < HEAD_DIM, qd, 0.0), extra], axis=1)
    dprob = lax.dot_general(
        left.astype(jnp.bfloat16), keys[...], NT, preferred_element_type=jnp.float32
    )
    slope = (weights.astype(jnp.float32) * dprob).astype(jnp.bfloat16)
    query_grad = jnp.dot(slope, keys[:, 0:128], preferred_element_type=jnp.float32)
    scaled = (qd * factor * jnp.where(lane < HEAD_DIM, 1.0, 0.125)).T.astype(jnp.bfloat16)
    value_acc[...] += jnp.dot(scaled[0:64], weights, preferred_element_type=jnp.float32)
    key_acc[...] += jnp.dot(scaled[64:128], slope, preferred_element_type=jnp.float32)
    return query_grad * (factor * 0.125)


def keep_mask(anchor, counter, row_ids, col_ids):
    mixed = (
        row_ids * jnp.int32(374761393)
        + col_ids * jnp.int32(668265263)
        + anchor * jnp.int32(1274126177)
        + counter
    )
    mixed = jnp.bitwise_xor(mixed, lax.shift_right_logical(mixed, jnp.full_like(mixed, 15)))
    mixed = mixed * jnp.int32(16777619)
    mixed = jnp.bitwise_xor(mixed, lax.shift_right_logical(mixed, jnp.full_like(mixed, 13)))
    mixed = mixed * jnp.int32(1274126177)
    mixed = jnp.bitwise_xor(mixed, lax.shift_right_logical(mixed, jnp.full_like(mixed, 16)))
    return (jnp.bitwise_and(mixed, jnp.int32(1023)) >= DROP_LEVEL).astype(jnp.float32)


def own_keep(seed_ref, rows, width):
    row_ids = lax.axis_index("ctx") * rows + lax.broadcasted_iota(jnp.int32, (rows, width), 0)
    col_ids = lax.axis_index("head") * width + lax.broadcasted_iota(jnp.int32, (rows, width), 1)
    return keep_mask(seed_ref[0], seed_ref[1], row_ids, col_ids)


def alive_column(tissue_ref):
    row = tissue_ref[...].astype(jnp.float32)
    return jnp.broadcast_to(row, (ROWS, ROWS)).T


def merged_tap(taps_ref, row, col, cols):
    tap = taps_ref[row * 7 + col : row * 7 + col + 1, cols]
    if 1 <= row <= 5 and 1 <= col <= 5:
        at = 49 + (row - 1) * 5 + col - 1
        tap = tap + taps_ref[at : at + 1, cols]
    if 2 <= row <= 4 and 2 <= col <= 4:
        at = 74 + (row - 2) * 3 + col - 2
        tap = tap + taps_ref[at : at + 1, cols]
    return tap


def depthwise(flipped, field, above, below, taps_ref, bias, padded):
    ctx = lax.axis_index("ctx")
    width = field.shape[1]
    grid_rows = ROWS // GRID_COLS
    has_above = jnp.where(ctx > 0, 1.0, 0.0)
    has_below = jnp.where(ctx < 63, 1.0, 0.0)
    field = field.astype(jnp.float32)
    padded[:, 0:8, :] = jnp.zeros((grid_rows + 6, 8, width), jnp.float32)
    padded[:, 40:48, :] = jnp.zeros((grid_rows + 6, 8, width), jnp.float32)
    padded[0:3, 8:40, :] = (above.astype(jnp.float32) * has_above).reshape(3, GRID_COLS, width)
    padded[3:7, 8:40, :] = field.reshape(grid_rows, GRID_COLS, width)
    padded[7:10, 8:40, :] = (below.astype(jnp.float32) * has_below).reshape(3, GRID_COLS, width)
    for start in range(0, width, 128):
        cols = slice(start, start + 128)
        total = field[:, cols].reshape(grid_rows, GRID_COLS, 128)
        if bias is not None:
            total = total + bias[:, cols].reshape(1, 1, 128)
        for col in range(7):
            moved = padded[:, 5 + col : 37 + col, cols]
            for row in range(7):
                if flipped:
                    tap = merged_tap(taps_ref, 6 - row, 6 - col, cols)
                else:
                    tap = merged_tap(taps_ref, row, col, cols)
                total = total + tap.reshape(1, 1, 128) * moved[row : row + grid_rows]
        yield cols, total.reshape(ROWS, 128)


def block_kernel(
    seed_ref,
    tokens_in,
    tissue_in,
    grad_in,
    taps_in,
    bias_in,
    gain_in,
    w_in,
    w_out_in,
    encoded_out,
    tokens_out,
    tokens,
    tissue,
    grad,
    taps,
    bias,
    gain,
    w,
    w_out,
    keep,
    masked,
    above,
    below,
    above_back,
    below_back,
    drop_full,
    full,
    query_part,
    grad_part,
    key_part,
    query_all,
    grad_all,
    key_all,
    keys,
    weights,
    attended,
    stats,
    value_acc,
    key_acc,
    query_out,
    out_out,
    key_out,
    query_back,
    out_back,
    key_back,
    grad_send,
    grad_recv,
    branch_send,
    branch_recv,
    sums_send,
    sums_recv,
    source,
    encoded,
    result,
    padded,
    send,
    recv,
    own,
    query_recv,
    grad_sem,
    key_recv,
    stat_send,
    stat_recv,
    query_back_send,
    query_back_recv,
    out_back_send,
    out_back_recv,
    key_back_recv,
):
    rows, width = tokens.shape
    ids = everyone()
    announce(ids)
    copies = Copies(send, recv, own)
    first = [
        copies.here(src, dst)
        for src, dst in ((tokens_in, tokens), (tissue_in, tissue), (grad_in, grad))
    ]
    for_conv = [copies.here(taps_in, taps), copies.here(bias_in, bias)]
    for_grad = [copies.here(w_out_in, w_out)]
    for_project = [copies.here(gain_in, gain), copies.here(w_in, w)]
    before, after = ring_ids()
    mine, heads = head_peers()
    q_mine, slot, q_peers = query_peers()
    k_mine, _, k_peers = key_peers()
    s_mine, s_peers = stat_peers()
    query_base = lax.axis_index("ctx") - q_mine
    keep[...] = own_keep(seed_ref, rows, width)
    for copy in first:
        copy.wait()
    alive = alive_column(tissue)
    column = alive[:, 0:1]
    masked[...] = (tokens[...].astype(jnp.float32) * column).astype(jnp.bfloat16)
    all_here(ids)
    halos = [
        copies.to(masked.at[pl.ds(32, 96)], above, {"ctx": after}),
        copies.to(masked.at[pl.ds(0, 96)], below, {"ctx": before}),
    ]
    upstream = grad[...].astype(jnp.float32) * column
    drop_full[mine] = (upstream * keep[...] * KEEP_SCALE).astype(jnp.bfloat16)
    drops = [copies.to(drop_full.at[mine], drop_full.at[mine], {"head": h}) for h in heads]

    for copy in for_grad:
        copy.wait()
    received(drops)
    out_grad = sum(
        lax.dot_general(
            drop_full[i],
            w_out[:, i * width : (i + 1) * width],
            NT,
            preferred_element_type=jnp.float32,
        )
        for i in range(QUADS)
    )
    for j in range(QUADS):
        pair = out_grad[:, 128 * (j // 2) : 128 * (j // 2) + 128]
        grad_part[j] = fold_rows(pair, j % 2 == 0).astype(jnp.bfloat16)
    for c, _, h in q_peers:
        copies.to(grad_part.at[h], grad_all.at[q_mine], {"ctx": c}, grad_sem.at[q_mine])
    grad_all[q_mine] = grad_part[slot]

    for copy in for_conv:
        copy.wait()
    received(halos)
    for cols, part in depthwise(
        False, masked[...], above[...], below[...], taps, bias[...].reshape(1, width), padded
    ):
        full[mine, :, cols] = (part * alive).astype(jnp.bfloat16)
    parts = [copies.to(full.at[mine], full.at[mine], {"head": h}) for h in heads]
    for copy in for_project:
        copy.wait()
    received(parts)
    unit, _ = normalised(full)
    gain_row = gain[...].reshape(1, QUADS * width)
    sums = [jnp.zeros((rows, w.shape[2]), jnp.float32) for _ in range(3)]
    for i in range(QUADS):
        span = slice(i * width, (i + 1) * width)
        normed = (unit[i] * gain_row[:, span]).astype(jnp.bfloat16)
        for k in range(3):
            sums[k] = sums[k] + jnp.dot(normed, w[k, span, :], preferred_element_type=jnp.float32)
    low = lanes(ROWS) < HEAD_DIM
    dead = alive == 0.0
    for j in range(QUADS):
        q, k, v = (part[:, 128 * (j // 2) : 128 * (j // 2) + 128] for part in sums)
        query_part[j] = fold_rows(q, j % 2 == 0).astype(jnp.bfloat16)
        if j % 2 == 0:
            both = jnp.where(low, v, pltpu.roll(k, 64, 1))
        else:
            both = jnp.where(low, pltpu.roll(v, 64, 1), k)
        key_part[j] = jnp.where(dead, DEAD, both).astype(jnp.bfloat16)
    for c, _, h in k_peers:
        copies.to(key_part.at[h], key_all.at[k_mine], {"ctx": c}, key_recv.at[k_mine])
    for c, _, h in q_peers:
        copies.to(query_part.at[h], query_all.at[q_mine], {"ctx": c}, query_recv.at[q_mine])
    query_all[q_mine] = query_part[slot]
    keys[rows_at(k_mine * ROWS, ROWS, ROWS), :] = key_block(key_part[slot])
    value_acc[...] = jnp.zeros_like(value_acc)
    key_acc[...] = jnp.zeros_like(key_acc)
    for c, at, _ in k_peers:
        arriving(key_all.at[at], send.at[0], key_recv.at[at], {"ctx": c}).wait_recv()
        keys[rows_at(at * ROWS, ROWS, ROWS), :] = key_block(key_all[at])

    def forward_step(step, _):
        chunk = mod(div(q_mine, 2) + step, CHUNKS)
        for half in range(2):
            at = 2 * chunk + half

            @pl.when(at != q_mine)
            def _(at=at):
                peer = {"ctx": query_base + at}
                arriving(grad_all.at[at], send.at[0], grad_sem.at[at], peer).wait_recv()
                arriving(query_all.at[at], send.at[0], query_recv.at[at], peer).wait_recv()

        qd = query_chunk(query_all, grad_all, chunk)
        rows_ = rows_at(chunk * CHUNK, CHUNK, CHUNK)
        stats[chunk, s_mine] = forward_chunk(qd, keys, weights, rows_, attended)
        for i, (c, _) in enumerate(s_peers):
            pltpu.make_async_remote_copy(
                src_ref=stats.at[chunk, s_mine],
                dst_ref=stats.at[chunk, s_mine],
                send_sem=stat_send.at[chunk, i],
                recv_sem=stat_recv.at[chunk, s_mine],
                device_id={"ctx": c},
                device_id_type=MESH,
            ).start()
        return 0

    lax.fori_loop(0, CHUNKS, forward_step, 0)

    def backward_step(step, _):
        chunk = mod(div(q_mine, 2) + step, CHUNKS)
        for c, at in s_peers:
            arriving(
                stats.at[chunk, at], send.at[0], stat_recv.at[chunk, at], {"ctx": c}
            ).wait_recv()
        share, shift, factor = chunk_columns(
            [stats[chunk, i] for i in range(4)], stats[chunk, s_mine]
        )
        qd = query_chunk(query_all, grad_all, chunk)
        rows_ = rows_at(chunk * CHUNK, CHUNK, CHUNK)
        query_grad = backward_chunk(
            qd, keys, weights[rows_, :], shift, factor, value_acc, key_acc
        )
        out = attended[rows_, :] * share
        for half in range(2):
            at = 2 * chunk + half
            span = slice(half * ROWS, (half + 1) * ROWS)
            query_out[at] = fold_rows(query_grad[span], False).astype(jnp.bfloat16)
            out_out[at] = fold_rows(out[span], True).astype(jnp.bfloat16)

            @pl.when(at != q_mine)
            def _(at=at):
                for src, dst, sent, got in (
                    (query_out, query_back, query_back_send, query_back_recv),
                    (out_out, out_back, out_back_send, out_back_recv),
                ):
                    pltpu.make_async_remote_copy(
                        src_ref=src.at[at],
                        dst_ref=dst.at[q_mine],
                        send_sem=sent.at[at],
                        recv_sem=got.at[q_mine],
                        device_id={"ctx": query_base + at},
                        device_id_type=MESH,
                    ).start()

        return 0

    lax.fori_loop(0, CHUNKS, backward_step, 0)
    for block in range(BLOCKS):
        cols = slice(block * ROWS, (block + 1) * ROWS)
        both = jnp.concatenate([value_acc[:, cols], key_acc[:, cols]], axis=0)
        key_out[block] = both.T.astype(jnp.bfloat16)
    for c, at, _ in k_peers:
        copies.to(key_out.at[at], key_back.at[k_mine], {"ctx": c}, key_back_recv.at[k_mine])
    key_back[k_mine] = key_out[k_mine]
    query_back[q_mine] = query_out[q_mine]
    out_back[q_mine] = out_out[q_mine]

    def total(ref, slots):
        parts = [ref[s].astype(jnp.float32) for s in slots]
        return (parts[0] + parts[1]) + (parts[2] + parts[3])

    def queries(ref):
        heads_ = []
        for j in range(QUADS):
            packed = total(ref, [8 * (j // 2) + 2 * k + j % 2 for k in range(4)])
            heads_.append(unfold_rows(packed, j % 2 == 0))
        pairs = [jnp.where(low, heads_[2 * p], heads_[2 * p + 1]) for p in range(2)]
        return jnp.concatenate(pairs, axis=1).astype(jnp.bfloat16)

    unit, spread = normalised(full)
    for c, at, _ in q_peers:
        arriving(out_back.at[at], send.at[0], out_back_recv.at[at], {"ctx": c}).wait_recv()
    out = queries(out_back)
    for i in range(QUADS):
        span = slice(i * width, (i + 1) * width)
        branch_send[i] = jnp.dot(
            out, w_out[:, span], preferred_element_type=jnp.float32
        ).astype(jnp.bfloat16)
    branches = [copies.to(branch_send.at[h], branch_recv.at[mine], {"head": h}) for h in heads]
    branch_recv[mine] = branch_send[mine]

    for c, at, _ in q_peers:
        arriving(query_back.at[at], send.at[0], query_back_recv.at[at], {"ctx": c}).wait_recv()
    query_sum = queries(query_back)
    for c, at, _ in k_peers:
        arriving(key_back.at[at], send.at[0], key_back_recv.at[at], {"ctx": c}).wait_recv()
    both = [total(key_back, [4 * k + j for k in range(4)]) for j in range(QUADS)]
    value_sum = [jnp.where(low, both[2 * p], pltpu.roll(both[2 * p + 1], 64, 1)) for p in range(2)]
    key_sum = [jnp.where(low, pltpu.roll(both[2 * p], 64, 1), both[2 * p + 1]) for p in range(2)]
    grads = [
        query_sum,
        jnp.concatenate(key_sum, axis=1).astype(jnp.bfloat16),
        jnp.concatenate(value_sum, axis=1).astype(jnp.bfloat16),
    ]
    plain = jnp.zeros((ROWS, 1), jnp.float32)
    crossed = jnp.zeros((ROWS, 1), jnp.float32)
    for i in range(QUADS):
        span = slice(i * width, (i + 1) * width)
        part = sum(
            lax.dot_general(grads[k], w[k, span, :], NT, preferred_element_type=jnp.float32)
            for k in range(3)
        )
        grad_send[i] = part.astype(jnp.bfloat16)
        scaled = part * gain_row[:, span]
        plain = plain + jnp.sum(scaled, axis=1, keepdims=True)
        crossed = crossed + jnp.sum(scaled * unit[i], axis=1, keepdims=True)
    lane = lanes(ROWS)
    sums_send[...] = jnp.where(lane == 0, plain, jnp.where(lane == 1, crossed, 0.0)).T[0:8]
    scattered = []
    for h in heads:
        scattered.append(copies.to(grad_send.at[h], grad_recv.at[mine], {"head": h}))
        scattered.append(copies.to(sums_send, sums_recv.at[mine], {"head": h}))
    grad_recv[mine] = grad_send[mine]
    sums_recv[mine] = sums_send[...]

    received(branches)
    branch = total(branch_recv, range(QUADS))
    residual = full[mine].astype(jnp.float32)
    encoded[...] = (residual + branch * keep[...] * KEEP_SCALE).astype(jnp.bfloat16)
    outs = [copies.here(encoded, encoded_out)]
    own_unit = jnp.zeros((ROWS, width), jnp.float32)
    own_gain = jnp.zeros((1, width), jnp.float32)
    for i in range(QUADS):
        own_unit = jnp.where(mine == i, unit[i], own_unit)
        own_gain = jnp.where(mine == i, gain_row[:, i * width : (i + 1) * width], own_gain)
    received(scattered)
    means = (sums_recv[0] + sums_recv[1]) + (sums_recv[2] + sums_recv[3])
    means = jnp.concatenate([means, jnp.zeros((120, 128), jnp.float32)], axis=0).T / (QUADS * width)
    scaled = total(grad_recv, range(QUADS)) * own_gain
    inner = scaled - means[:, 0:1] - own_unit * means[:, 1:2]
    column = alive_column(tissue)[:, 0:1]
    upstream = grad[...].astype(jnp.float32) * column
    source[...] = ((upstream + inner * spread) * column).astype(jnp.bfloat16)
    halos = [
        copies.to(source.at[pl.ds(32, 96)], above_back, {"ctx": after}),
        copies.to(source.at[pl.ds(0, 96)], below_back, {"ctx": before}),
    ]
    received(halos)
    for cols, part in depthwise(
        True, source[...], above_back[...], below_back[...], taps, None, padded
    ):
        result[:, cols] = part.astype(jnp.bfloat16)
    outs.append(copies.here(result, tokens_out))

    copies.sent()
    for chunk in range(CHUNKS):
        for i, (c, _) in enumerate(s_peers):
            tile = stats.at[chunk, s_mine]
            arriving(tile, stat_send.at[chunk, i], stat_recv.at[chunk, s_mine], {"ctx": c}).wait_send()
    for c, at, _ in q_peers:
        peer = {"ctx": c}
        arriving(query_out.at[at], query_back_send.at[at], query_back_recv.at[at], peer).wait_send()
        arriving(out_out.at[at], out_back_send.at[at], out_back_recv.at[at], peer).wait_send()
    for copy in outs:
        copy.wait()


def on_device(tokens, tissue, conv_taps, conv_bias, ln_gain, w_qkv, w_out, drop_seed, grad_out):
    rows, width = tokens.shape
    args = [
        tokens,
        tissue[None, :],
        grad_out,
        conv_taps,
        conv_bias,
        ln_gain,
        w_qkv.transpose(1, 0, 2),
        w_out,
    ]
    far = 2 + 3 + 15 + 3 + 15 + 15 + 15 + 3 + 6 + 2

    def held(*shape, dtype=jnp.bfloat16):
        return pltpu.VMEM(shape, dtype)

    def sems(*shape):
        return pltpu.SemaphoreType.DMA(shape)

    f32 = jnp.float32
    quads = held(QUADS, rows, width)
    halves = held(BLOCKS, HALF, 128)
    wholes = held(BLOCKS, ROWS, 128)
    halo = held(96, width)
    own = held(rows, width)
    scratch = [pltpu.VMEM(a.shape, a.dtype) for a in args]
    scratch += [held(rows, width, dtype=f32), own, halo, halo, halo, halo, quads, quads]
    scratch += [held(QUADS, HALF, 128), held(QUADS, HALF, 128), held(QUADS, ROWS, 128)]
    scratch += [halves, halves, wholes, held(SPAN, 256), held(SPAN, SPAN)]
    scratch += [held(SPAN, 128, dtype=f32), held(CHUNKS, 4, 8, 128, dtype=f32)]
    scratch += [held(HEAD_DIM, SPAN, dtype=f32), held(HEAD_DIM, SPAN, dtype=f32)]
    scratch += [halves, halves, wholes, halves, halves, wholes]
    scratch += [quads, quads, quads, quads, held(8, rows, dtype=f32), held(QUADS, 8, rows, dtype=f32)]
    scratch += [own, own, own, held(rows // GRID_COLS + 6, 48, width, dtype=f32)]
    scratch += [sems(far), sems(far), sems(10), sems(BLOCKS), sems(BLOCKS), sems(BLOCKS)]
    scratch += [sems(CHUNKS, 3), sems(CHUNKS, 4)] + [sems(BLOCKS)] * 5
    encoded, grad_tokens = pl.pallas_call(
        block_kernel,
        out_shape=[struct((rows, width))] * 2,
        in_specs=[pl.BlockSpec(memory_space=pltpu.SMEM)] + [ANY] * len(args),
        out_specs=[ANY] * 2,
        scratch_shapes=scratch,
        compiler_params=pltpu.CompilerParams(
            collective_id=1, has_side_effects=True, vmem_limit_bytes=WHOLE
        ),
    )(drop_seed, *args)
    alive = tissue.astype(jnp.bfloat16)[:, None]
    return (encoded * alive, grad_tokens * alive)


def solution(mesh):
    placed = (
        P("ctx", "head"),
        P("ctx"),
        P(None, "head"),
        P("head"),
        P(),
        P(None, None, "head"),
        P("head", None),
        P(),
        P("ctx", "head"),
    )
    return jax.shard_map(
        on_device,
        mesh=mesh,
        in_specs=placed,
        out_specs=(P("ctx", "head"), P("ctx", "head")),
        check_vma=False,
    )
```

```python
import jax
import jax.numpy as jnp
from jax import lax
from jax.experimental import pallas as pl
from jax.experimental.pallas import tpu as pltpu
from jax.sharding import PartitionSpec as P

HEAD_DIM = 64
GRID_COLS = 32
ROWS = 128
QUADS = 4
BLOCKS = 16
SPAN = BLOCKS * ROWS
CHUNK = 512
HALF = ROWS // 2
WHOLE = 60 << 20
CHUNKS = SPAN // CHUNK
PER = CHUNK // ROWS
TILE = (3 * PER + 7) // 8 * 8

DROP_LEVEL = 103
KEEP_SCALE = 1024.0 / 921.0
NEG = -1e30
EPS = 1e-05
DEAD = 2.0**100

MESH = pl.DeviceIdType.MESH
ANY = pl.BlockSpec(memory_space=pl.ANY)
NT = (((1,), (1,)), ((), ()))


def struct(shape, dtype=jnp.bfloat16):
    return jax.ShapeDtypeStruct(shape, dtype)


def div(a, b):
    return lax.div(a, jnp.int32(b))


def mod(a, b):
    return lax.rem(a, jnp.int32(b))


def place():
    ctx = lax.axis_index("ctx")
    return ctx, div(ctx, 16), mod(div(ctx, 8), 2), mod(ctx, 8)


def query_peers():
    ctx, x, y, z = place()
    mine = mod(ctx, 16)
    peers = []
    for up, over in ((1, 4), (1, 3), (1, 5), (0, 4), (1, 2), (1, 6), (0, 3), (0, 5)) + (
        (1, 1), (1, 7), (0, 2), (0, 6), (1, 0), (0, 1), (0, 7)
    ):
        to_y, to_z = mod(y + up, 2), mod(z + over, 8)
        to = to_y * 8 + to_z
        peers.append((x * 16 + to, to, 2 * to_y + mod(to_z, 2)))
    return mine, 2 * y + mod(z, 2), peers


def key_peers():
    ctx, x, y, z = place()
    bit = mod(z, 2)
    mine = x * 4 + y * 2 + bit
    peers = []
    for side, up, over in ((2, 1, 1), (2, 1, 0), (1, 1, 1), (3, 1, 1), (1, 1, 0), (3, 1, 0)) + (
        (2, 0, 1), (0, 1, 1), (2, 0, 0), (0, 1, 0), (1, 0, 1), (3, 0, 1), (1, 0, 0), (3, 0, 0), (0, 0, 1)
    ):
        to_x, to_y, to_bit = mod(x + side, 4), mod(y + up, 2), mod(bit + over, 2)
        to = to_x * 4 + to_y * 2 + to_bit
        peers.append((to_x * 16 + to_y * 8 + z - bit + to_bit, to, to_y * 2 + to_bit))
    return mine, 2 * y + bit, peers


def stat_peers():
    ctx, x, y, z = place()
    mine = div(z, 2)
    base = ctx - z + mod(z, 2)
    peers = []
    for step in range(1, 4):
        to = mod(mine + step, 4)
        peers.append((base + to * 2, to))
    return mine, peers


def head_peers():
    mine = lax.axis_index("head")
    return mine, [mod(mine + step, 4) for step in range(1, 4)]


class Copies:
    def __init__(self, send, recv, own):
        self.send, self.recv, self.own = send, recv, own
        self.far, self.near = [], []

    def to(self, src, dst, device, recv=None):
        at = len(self.far)
        copy = pltpu.make_async_remote_copy(
            src_ref=src,
            dst_ref=dst,
            send_sem=self.send.at[at],
            recv_sem=self.recv.at[at] if recv is None else recv,
            device_id=device,
            device_id_type=MESH,
        )
        copy.start()
        self.far.append(copy)
        return copy

    def here(self, src, dst):
        copy = pltpu.make_async_copy(src, dst, self.own.at[len(self.near)])
        copy.start()
        self.near.append(copy)
        return copy

    def sent(self):
        for copy in self.far:
            copy.wait_send()


def received(copies):
    for copy in copies:
        copy.wait_recv()


def arriving(slot, send, recv, device):
    return pltpu.make_async_remote_copy(
        src_ref=slot,
        dst_ref=slot,
        send_sem=send,
        recv_sem=recv,
        device_id=device,
        device_id_type=MESH,
    )


def ring_ids():
    ctx = lax.axis_index("ctx")
    return mod(ctx + 63, 64), mod(ctx + 1, 64)


def everyone():
    ids = []
    for (q, _, _), (k, _, _) in zip(query_peers()[2], key_peers()[2]):
        ids += [{"ctx": q}, {"ctx": k}]
    before, after = ring_ids()
    return ids + [{"ctx": before}, {"ctx": after}] + [{"head": h} for h in head_peers()[1]]


class Halo:
    def __init__(self, field, above, below, send, recv):
        self.ctx = lax.axis_index("ctx")
        before, after = ring_ids()
        self.above, self.below = above, below
        self.down, self.up = [], []
        for tile in range(field.shape[1] // 128):
            cols = pl.ds(tile * 128, 128)
            for side, (rows, dst, to, list_) in enumerate(
                ((32, above, after, self.down), (0, below, before, self.up))
            ):
                list_.append(
                    pltpu.make_async_remote_copy(
                        src_ref=field.at[pl.ds(rows, 96), cols],
                        dst_ref=dst.at[:, cols],
                        send_sem=send.at[side, tile],
                        recv_sem=recv.at[side, tile],
                        device_id={"ctx": to},
                        device_id_type=MESH,
                    )
                )

    def clear(self):
        @pl.when(self.ctx == 0)
        def _():
            self.above[...] = jnp.zeros_like(self.above)

        @pl.when(self.ctx == 63)
        def _():
            self.below[...] = jnp.zeros_like(self.below)

    def start(self):
        @pl.when(self.ctx < 63)
        def _():
            for copy in self.down:
                copy.start()

        @pl.when(self.ctx > 0)
        def _():
            for copy in self.up:
                copy.start()

    def ready(self, tile):
        @pl.when(self.ctx > 0)
        def _():
            self.down[tile].wait_recv()

        @pl.when(self.ctx < 63)
        def _():
            self.up[tile].wait_recv()

    def sent(self):
        @pl.when(self.ctx < 63)
        def _():
            for copy in self.down:
                copy.wait_send()

        @pl.when(self.ctx > 0)
        def _():
            for copy in self.up:
                copy.wait_send()


def announce(ids):
    barrier = pltpu.get_barrier_semaphore()
    for device in ids:
        pl.semaphore_signal(barrier, inc=1, device_id=device, device_id_type=MESH)


def all_here(ids):
    pl.semaphore_wait(pltpu.get_barrier_semaphore(), len(ids))


def lanes(rows, width=128):
    return lax.broadcasted_iota(jnp.int32, (rows, width), 1)


def normalised(full_ref):
    parts = [full_ref[i].astype(jnp.float32) for i in range(QUADS)]
    width = QUADS * parts[0].shape[1]
    mean = sum(jnp.sum(p, axis=1, keepdims=True) for p in parts) / width
    parts = [p - mean for p in parts]
    var = sum(jnp.sum(p * p, axis=1, keepdims=True) for p in parts) / width
    spread = lax.rsqrt(var + EPS)
    return [p * spread for p in parts], spread


def fold(top, bottom, low_half):
    low = lanes(top.shape[0]) < HEAD_DIM
    if low_half:
        return jnp.where(low, top, pltpu.roll(bottom, 64, 1))
    return jnp.where(low, pltpu.roll(top, 64, 1), bottom)


def fold_rows(block, low_half):
    return fold(block[0:64], block[64:128], low_half)


def unfold_rows(packed, low_half):
    moved = pltpu.roll(packed, 64, 1)
    return jnp.concatenate([packed, moved] if low_half else [moved, packed], axis=0)


def query_chunk(q_ref, d_ref, at):
    blocks = []
    for block in range(PER):
        q = unfold_rows(q_ref[PER * at + block].astype(jnp.float32), False)
        d = unfold_rows(d_ref[PER * at + block].astype(jnp.float32), True)
        blocks.append(jnp.where(lanes(ROWS) < HEAD_DIM, d, q))
    return jnp.concatenate(blocks, axis=0)


def key_block(part):
    part = part.astype(jnp.float32)
    alive = part[:, 0:1] < DEAD / 2
    lane = lanes(ROWS)
    extra = jnp.where(lane == 0, jnp.where(alive, 0.0, NEG), jnp.where(lane < 4, 1.0, 0.0))
    return jnp.concatenate([jnp.where(alive, part, 0.0), extra], axis=1).astype(jnp.bfloat16)


def rows_at(start, count_, multiple):
    return pl.ds(pl.multiple_of(start, multiple), count_)


def scores_of(qd, keys):
    lane = lanes(qd.shape[0])
    left = jnp.concatenate(
        [jnp.where(lane >= HEAD_DIM, qd * 0.125, 0.0), jnp.where(lane == 0, 1.0, 0.0)], axis=1
    ).astype(jnp.bfloat16)
    return lax.dot_general(left, keys, NT, preferred_element_type=jnp.float32)


def forward_chunk(qd, keys, weights, rows, attended):
    lane = lanes(CHUNK)
    scores = scores_of(qd, keys[...])
    highest = jnp.max(scores, axis=1, keepdims=True)
    part = jnp.exp(scores - highest).astype(jnp.bfloat16)
    weights[rows, :] = part
    summed = jnp.dot(part, keys[...], preferred_element_type=jnp.float32)
    totals = summed[:, 129:130]
    mine = summed[:, 0:128] / totals
    attended[rows, :] = mine
    inner = jnp.sum(jnp.where(lane < HEAD_DIM, mine * qd, 0.0), axis=1, keepdims=True)
    log_total = highest + jnp.log(totals)
    table = jnp.where(
        lane == 0, log_total, jnp.where(lane == 1, inner, jnp.where(lane == 2, highest, 0.0))
    ).T
    parts = [table[k : k + 1, h * ROWS : (h + 1) * ROWS] for k in range(3) for h in range(PER)]
    return jnp.concatenate(parts + [jnp.zeros((TILE - 3 * PER, 128), jnp.float32)], axis=0)


def chunk_columns(stats, mine):
    logs = [stats[i][0:PER] for i in range(4)]
    top = jnp.maximum(jnp.maximum(logs[0], logs[1]), jnp.maximum(logs[2], logs[3]))
    total = top + jnp.log(sum(jnp.exp(part - top) for part in logs))
    shift = sum(jnp.exp(logs[i] - total) * stats[i][PER : 2 * PER] for i in range(4))
    share = jnp.exp(mine[0:PER] - total)
    factor = jnp.exp(mine[2 * PER : 3 * PER] - total)
    rest = jnp.zeros((128 - 3 * PER, 128), jnp.float32)
    rows = jnp.concatenate([share, shift, factor, rest], axis=0).T
    return [
        jnp.concatenate([rows[:, k * PER + h : k * PER + h + 1] for h in range(PER)], axis=0)
        for k in range(3)
    ]


def backward_chunk(qd, keys, weights, shift, factor, value_acc, key_acc):
    lane = lanes(CHUNK)
    high = shift.astype(jnp.bfloat16).astype(jnp.float32)
    middle = (shift - high).astype(jnp.bfloat16).astype(jnp.float32)
    low = shift - high - middle
    extra = jnp.where(
        lane == 1, -high, jnp.where(lane == 2, -middle, jnp.where(lane == 3, -low, 0.0))
    )
    left = jnp.concatenate([jnp.where(lane < HEAD_DIM, qd, 0.0), extra], axis=1)
    dprob = lax.dot_general(
        left.astype(jnp.bfloat16), keys[...], NT, preferred_element_type=jnp.float32
    )
    slope = (weights.astype(jnp.float32) * dprob).astype(jnp.bfloat16)
    query_grad = jnp.dot(slope, keys[:, 0:128], preferred_element_type=jnp.float32)
    scaled = (qd * factor * jnp.where(lane < HEAD_DIM, 1.0, 0.125)).T.astype(jnp.bfloat16)
    value_acc[...] += jnp.dot(scaled[0:64], weights, preferred_element_type=jnp.float32)
    key_acc[...] += jnp.dot(scaled[64:128], slope, preferred_element_type=jnp.float32)
    return query_grad * (factor * 0.125)


def keep_mask(anchor, counter, row_ids, col_ids):
    mixed = (
        row_ids * jnp.int32(374761393)
        + col_ids * jnp.int32(668265263)
        + anchor * jnp.int32(1274126177)
        + counter
    )
    mixed = jnp.bitwise_xor(mixed, lax.shift_right_logical(mixed, jnp.full_like(mixed, 15)))
    mixed = mixed * jnp.int32(16777619)
    mixed = jnp.bitwise_xor(mixed, lax.shift_right_logical(mixed, jnp.full_like(mixed, 13)))
    mixed = mixed * jnp.int32(1274126177)
    mixed = jnp.bitwise_xor(mixed, lax.shift_right_logical(mixed, jnp.full_like(mixed, 16)))
    return (jnp.bitwise_and(mixed, jnp.int32(1023)) >= DROP_LEVEL).astype(jnp.float32)


def own_keep(seed_ref, rows, width):
    row_ids = lax.axis_index("ctx") * rows + lax.broadcasted_iota(jnp.int32, (rows, width), 0)
    col_ids = lax.axis_index("head") * width + lax.broadcasted_iota(jnp.int32, (rows, width), 1)
    return keep_mask(seed_ref[0], seed_ref[1], row_ids, col_ids)


def alive_column(tissue_ref):
    row = tissue_ref[...].astype(jnp.float32)
    return jnp.broadcast_to(row, (ROWS, ROWS)).T


def merged_tap(taps_ref, row, col, cols):
    tap = taps_ref[row * 7 + col : row * 7 + col + 1, cols]
    if 1 <= row <= 5 and 1 <= col <= 5:
        at = 49 + (row - 1) * 5 + col - 1
        tap = tap + taps_ref[at : at + 1, cols]
    if 2 <= row <= 4 and 2 <= col <= 4:
        at = 74 + (row - 2) * 3 + col - 2
        tap = tap + taps_ref[at : at + 1, cols]
    return tap


def depthwise(flipped, field_ref, halo, taps_ref, bias, padded):
    width = field_ref.shape[1]
    grid_rows = ROWS // GRID_COLS
    padded[3:7, 8:40, :] = field_ref[...].astype(jnp.float32).reshape(grid_rows, GRID_COLS, width)
    for tile in range(width // 128):
        cols = slice(tile * 128, tile * 128 + 128)
        total = padded[3:7, 8:40, cols]
        if bias is not None:
            total = total + bias[:, cols].reshape(1, 1, 128)
        halo.ready(tile)
        for start, ref in ((0, halo.above), (7, halo.below)):
            part = ref[:, cols].astype(jnp.float32)
            padded[start : start + 3, 8:40, cols] = part.reshape(3, GRID_COLS, 128)
        for col in range(7):
            moved = padded[:, 5 + col : 37 + col, cols]
            for row in range(7):
                if flipped:
                    tap = merged_tap(taps_ref, 6 - row, 6 - col, cols)
                else:
                    tap = merged_tap(taps_ref, row, col, cols)
                total = total + tap.reshape(1, 1, 128) * moved[row : row + grid_rows]
        yield cols, total.reshape(ROWS, 128)


def block_kernel(
    seed_ref,
    tokens_in,
    tissue_in,
    grad_in,
    taps_in,
    bias_in,
    gain_in,
    w_in,
    w_out_in,
    encoded_out,
    tokens_out,
    tokens,
    tissue,
    grad,
    taps,
    bias,
    gain,
    w,
    w_out,
    keep,
    masked,
    above,
    below,
    above_back,
    below_back,
    drop_full,
    full,
    query_part,
    grad_part,
    key_part,
    query_all,
    grad_all,
    key_all,
    keys,
    weights,
    attended,
    stats,
    value_acc,
    key_acc,
    query_out,
    out_out,
    key_out,
    query_back,
    out_back,
    key_back,
    grad_send,
    grad_recv,
    branch_send,
    branch_recv,
    sums_send,
    sums_recv,
    source,
    encoded,
    result,
    padded,
    send,
    recv,
    own,
    query_recv,
    grad_sem,
    key_recv,
    stat_send,
    stat_recv,
    query_back_send,
    query_back_recv,
    out_back_send,
    out_back_recv,
    key_back_recv,
    halo_send,
    halo_recv,
    halo_back_send,
    halo_back_recv,
):
    rows, width = tokens.shape
    ids = everyone()
    announce(ids)
    copies = Copies(send, recv, own)
    first = [
        copies.here(src, dst)
        for src, dst in ((tokens_in, tokens), (tissue_in, tissue), (grad_in, grad))
    ]
    for_conv = [copies.here(taps_in, taps), copies.here(bias_in, bias)]
    for_grad = [copies.here(w_out_in, w_out)]
    for_project = [copies.here(gain_in, gain), copies.here(w_in, w)]
    mine, heads = head_peers()
    q_mine, slot, q_peers = query_peers()
    k_mine, _, k_peers = key_peers()
    s_mine, s_peers = stat_peers()
    query_base = lax.axis_index("ctx") - q_mine
    halo = Halo(masked, above, below, halo_send, halo_recv)
    halo_back = Halo(source, above_back, below_back, halo_back_send, halo_back_recv)
    halo.clear()
    halo_back.clear()
    padded[:, 0:8, :] = jnp.zeros((padded.shape[0], 8, width), jnp.float32)
    padded[:, 40:48, :] = jnp.zeros((padded.shape[0], 8, width), jnp.float32)
    keep[...] = own_keep(seed_ref, rows, width)
    for copy in first:
        copy.wait()
    alive = alive_column(tissue)
    column = alive[:, 0:1]
    masked[...] = (tokens[...].astype(jnp.float32) * column).astype(jnp.bfloat16)
    all_here(ids)
    halo.start()
    upstream = grad[...].astype(jnp.float32) * column
    drop_full[mine] = (upstream * keep[...] * KEEP_SCALE).astype(jnp.bfloat16)
    drops = [copies.to(drop_full.at[mine], drop_full.at[mine], {"head": h}) for h in heads]

    for copy in for_conv:
        copy.wait()
    for cols, part in depthwise(False, masked, halo, taps, bias[...].reshape(1, width), padded):
        full[mine, :, cols] = (part * alive).astype(jnp.bfloat16)
    parts = [copies.to(full.at[mine], full.at[mine], {"head": h}) for h in heads]

    for copy in for_grad:
        copy.wait()
    received(drops)
    out_grad = sum(
        lax.dot_general(
            drop_full[i],
            w_out[:, i * width : (i + 1) * width],
            NT,
            preferred_element_type=jnp.float32,
        )
        for i in range(QUADS)
    )
    for j in range(QUADS):
        pair = out_grad[:, 128 * (j // 2) : 128 * (j // 2) + 128]
        grad_part[j] = fold_rows(pair, j % 2 == 0).astype(jnp.bfloat16)
    for c, _, h in q_peers:
        copies.to(grad_part.at[h], grad_all.at[q_mine], {"ctx": c}, grad_sem.at[q_mine])
    grad_all[q_mine] = grad_part[slot]

    for copy in for_project:
        copy.wait()
    received(parts)
    unit, _ = normalised(full)
    gain_row = gain[...].reshape(1, QUADS * width)
    sums = [jnp.zeros((rows, w.shape[2]), jnp.float32) for _ in range(3)]
    for i in range(QUADS):
        span = slice(i * width, (i + 1) * width)
        normed = (unit[i] * gain_row[:, span]).astype(jnp.bfloat16)
        for k in range(3):
            sums[k] = sums[k] + jnp.dot(normed, w[k, span, :], preferred_element_type=jnp.float32)
    low = lanes(ROWS) < HEAD_DIM
    dead = alive == 0.0
    for j in range(QUADS):
        q, k, v = (part[:, 128 * (j // 2) : 128 * (j // 2) + 128] for part in sums)
        query_part[j] = fold_rows(q, j % 2 == 0).astype(jnp.bfloat16)
        if j % 2 == 0:
            both = jnp.where(low, v, pltpu.roll(k, 64, 1))
        else:
            both = jnp.where(low, pltpu.roll(v, 64, 1), k)
        key_part[j] = jnp.where(dead, DEAD, both).astype(jnp.bfloat16)
    for c, _, h in k_peers:
        copies.to(key_part.at[h], key_all.at[k_mine], {"ctx": c}, key_recv.at[k_mine])
    for c, _, h in q_peers:
        copies.to(query_part.at[h], query_all.at[q_mine], {"ctx": c}, query_recv.at[q_mine])
    query_all[q_mine] = query_part[slot]
    keys[rows_at(k_mine * ROWS, ROWS, ROWS), :] = key_block(key_part[slot])
    value_acc[...] = jnp.zeros_like(value_acc)
    key_acc[...] = jnp.zeros_like(key_acc)
    for c, at, _ in k_peers:
        arriving(key_all.at[at], send.at[0], key_recv.at[at], {"ctx": c}).wait_recv()
        keys[rows_at(at * ROWS, ROWS, ROWS), :] = key_block(key_all[at])

    def chunk_at(step):
        return mod(div(q_mine, PER) + 1 + step, CHUNKS)

    def forward_step(step, _):
        chunk = chunk_at(step)
        for half in range(PER):
            at = PER * chunk + half

            @pl.when(at != q_mine)
            def _(at=at):
                peer = {"ctx": query_base + at}
                arriving(grad_all.at[at], send.at[0], grad_sem.at[at], peer).wait_recv()
                arriving(query_all.at[at], send.at[0], query_recv.at[at], peer).wait_recv()

        qd = query_chunk(query_all, grad_all, chunk)
        stats[chunk, s_mine] = forward_chunk(
            qd, keys, weights, rows_at(chunk * CHUNK, CHUNK, CHUNK), attended
        )
        for i, (c, _) in enumerate(s_peers):
            pltpu.make_async_remote_copy(
                src_ref=stats.at[chunk, s_mine],
                dst_ref=stats.at[chunk, s_mine],
                send_sem=stat_send.at[chunk, i],
                recv_sem=stat_recv.at[chunk, s_mine],
                device_id={"ctx": c},
                device_id_type=MESH,
            ).start()
        return 0

    lax.fori_loop(0, CHUNKS, forward_step, 0)

    def backward_step(step, _):
        chunk = chunk_at(step)
        for c, at in s_peers:
            arriving(
                stats.at[chunk, at], send.at[0], stat_recv.at[chunk, at], {"ctx": c}
            ).wait_recv()
        share, shift, factor = chunk_columns(
            [stats[chunk, i] for i in range(4)], stats[chunk, s_mine]
        )
        qd = query_chunk(query_all, grad_all, chunk)
        rows_ = rows_at(chunk * CHUNK, CHUNK, CHUNK)
        query_grad = backward_chunk(
            qd, keys, weights[rows_, :], shift, factor, value_acc, key_acc
        )
        out = attended[rows_, :] * share
        for half in range(PER):
            at = PER * chunk + half
            span = slice(half * ROWS, (half + 1) * ROWS)
            query_out[at] = fold_rows(query_grad[span], False).astype(jnp.bfloat16)
            out_out[at] = fold_rows(out[span], True).astype(jnp.bfloat16)

            @pl.when(at != q_mine)
            def _(at=at):
                for src, dst, sent, got in (
                    (query_out, query_back, query_back_send, query_back_recv),
                    (out_out, out_back, out_back_send, out_back_recv),
                ):
                    pltpu.make_async_remote_copy(
                        src_ref=src.at[at],
                        dst_ref=dst.at[q_mine],
                        send_sem=sent.at[at],
                        recv_sem=got.at[q_mine],
                        device_id={"ctx": query_base + at},
                        device_id_type=MESH,
                    ).start()

        return 0

    lax.fori_loop(0, CHUNKS, backward_step, 0)
    for block in range(BLOCKS):
        cols = slice(block * ROWS, (block + 1) * ROWS)
        both = jnp.concatenate([value_acc[:, cols], key_acc[:, cols]], axis=0)
        key_out[block] = both.T.astype(jnp.bfloat16)
    for c, at, _ in k_peers:
        copies.to(key_out.at[at], key_back.at[k_mine], {"ctx": c}, key_back_recv.at[k_mine])
    key_back[k_mine] = key_out[k_mine]
    query_back[q_mine] = query_out[q_mine]
    out_back[q_mine] = out_out[q_mine]

    def total(ref, slots):
        parts = [ref[s].astype(jnp.float32) for s in slots]
        return (parts[0] + parts[1]) + (parts[2] + parts[3])

    def queries(ref):
        heads_ = []
        for j in range(QUADS):
            packed = total(ref, [8 * (j // 2) + 2 * k + j % 2 for k in range(4)])
            heads_.append(unfold_rows(packed, j % 2 == 0))
        pairs = [jnp.where(low, heads_[2 * p], heads_[2 * p + 1]) for p in range(2)]
        return jnp.concatenate(pairs, axis=1).astype(jnp.bfloat16)

    unit, spread = normalised(full)
    for c, at, _ in q_peers:
        arriving(out_back.at[at], send.at[0], out_back_recv.at[at], {"ctx": c}).wait_recv()
    out = queries(out_back)
    for i in range(QUADS):
        span = slice(i * width, (i + 1) * width)
        branch_send[i] = jnp.dot(
            out, w_out[:, span], preferred_element_type=jnp.float32
        ).astype(jnp.bfloat16)
    branches = [copies.to(branch_send.at[h], branch_recv.at[mine], {"head": h}) for h in heads]
    branch_recv[mine] = branch_send[mine]

    for c, at, _ in q_peers:
        arriving(query_back.at[at], send.at[0], query_back_recv.at[at], {"ctx": c}).wait_recv()
    query_sum = queries(query_back)
    for c, at, _ in k_peers:
        arriving(key_back.at[at], send.at[0], key_back_recv.at[at], {"ctx": c}).wait_recv()
    both = [total(key_back, [4 * k + j for k in range(4)]) for j in range(QUADS)]
    value_sum = [jnp.where(low, both[2 * p], pltpu.roll(both[2 * p + 1], 64, 1)) for p in range(2)]
    key_sum = [jnp.where(low, pltpu.roll(both[2 * p], 64, 1), both[2 * p + 1]) for p in range(2)]
    grads = [
        query_sum,
        jnp.concatenate(key_sum, axis=1).astype(jnp.bfloat16),
        jnp.concatenate(value_sum, axis=1).astype(jnp.bfloat16),
    ]
    plain = jnp.zeros((ROWS, 1), jnp.float32)
    crossed = jnp.zeros((ROWS, 1), jnp.float32)
    for i in range(QUADS):
        span = slice(i * width, (i + 1) * width)
        part = sum(
            lax.dot_general(grads[k], w[k, span, :], NT, preferred_element_type=jnp.float32)
            for k in range(3)
        )
        grad_send[i] = part.astype(jnp.bfloat16)
        scaled = part * gain_row[:, span]
        plain = plain + jnp.sum(scaled, axis=1, keepdims=True)
        crossed = crossed + jnp.sum(scaled * unit[i], axis=1, keepdims=True)
    lane = lanes(ROWS)
    sums_send[...] = jnp.where(lane == 0, plain, jnp.where(lane == 1, crossed, 0.0)).T[0:8]
    scattered = []
    for h in heads:
        scattered.append(copies.to(grad_send.at[h], grad_recv.at[mine], {"head": h}))
        scattered.append(copies.to(sums_send, sums_recv.at[mine], {"head": h}))
    grad_recv[mine] = grad_send[mine]
    sums_recv[mine] = sums_send[...]

    received(branches)
    branch = total(branch_recv, range(QUADS))
    residual = full[mine].astype(jnp.float32)
    encoded[...] = (residual + branch * keep[...] * KEEP_SCALE).astype(jnp.bfloat16)
    outs = [copies.here(encoded, encoded_out)]
    own_unit = jnp.zeros((ROWS, width), jnp.float32)
    own_gain = jnp.zeros((1, width), jnp.float32)
    for i in range(QUADS):
        own_unit = jnp.where(mine == i, unit[i], own_unit)
        own_gain = jnp.where(mine == i, gain_row[:, i * width : (i + 1) * width], own_gain)
    received(scattered)
    means = (sums_recv[0] + sums_recv[1]) + (sums_recv[2] + sums_recv[3])
    means = jnp.concatenate([means, jnp.zeros((120, 128), jnp.float32)], axis=0).T / (QUADS * width)
    scaled = total(grad_recv, range(QUADS)) * own_gain
    inner = scaled - means[:, 0:1] - own_unit * means[:, 1:2]
    column = alive_column(tissue)[:, 0:1]
    upstream = grad[...].astype(jnp.float32) * column
    source[...] = ((upstream + inner * spread) * column).astype(jnp.bfloat16)
    halo_back.start()
    for cols, part in depthwise(True, source, halo_back, taps, None, padded):
        result[:, cols] = part.astype(jnp.bfloat16)
    outs.append(copies.here(result, tokens_out))

    halo.sent()
    halo_back.sent()
    copies.sent()
    for chunk in range(CHUNKS):
        for i, (c, _) in enumerate(s_peers):
            tile = stats.at[chunk, s_mine]
            arriving(tile, stat_send.at[chunk, i], stat_recv.at[chunk, s_mine], {"ctx": c}).wait_send()
    for c, at, _ in q_peers:
        peer = {"ctx": c}
        arriving(query_out.at[at], query_back_send.at[at], query_back_recv.at[at], peer).wait_send()
        arriving(out_out.at[at], out_back_send.at[at], out_back_recv.at[at], peer).wait_send()
    for copy in outs:
        copy.wait()


def on_device(tokens, tissue, conv_taps, conv_bias, ln_gain, w_qkv, w_out, drop_seed, grad_out):
    rows, width = tokens.shape
    args = [
        tokens,
        tissue[None, :],
        grad_out,
        conv_taps,
        conv_bias,
        ln_gain,
        w_qkv.transpose(1, 0, 2),
        w_out,
    ]
    far = 3 + 15 + 3 + 15 + 15 + 15 + 3 + 6

    def held(*shape, dtype=jnp.bfloat16):
        return pltpu.VMEM(shape, dtype)

    def sems(*shape):
        return pltpu.SemaphoreType.DMA(shape)

    f32 = jnp.float32
    quads = held(QUADS, rows, width)
    halves = held(BLOCKS, HALF, 128)
    wholes = held(BLOCKS, ROWS, 128)
    halo = held(96, width)
    own = held(rows, width)
    scratch = [pltpu.VMEM(a.shape, a.dtype) for a in args]
    scratch += [held(rows, width, dtype=f32), own, halo, halo, halo, halo, quads, quads]
    scratch += [held(QUADS, HALF, 128), held(QUADS, HALF, 128), held(QUADS, ROWS, 128)]
    scratch += [halves, halves, wholes, held(SPAN, 256), held(SPAN, SPAN)]
    scratch += [held(SPAN, 128, dtype=f32), held(CHUNKS, 4, TILE, 128, dtype=f32)]
    scratch += [held(HEAD_DIM, SPAN, dtype=f32), held(HEAD_DIM, SPAN, dtype=f32)]
    scratch += [halves, halves, wholes, halves, halves, wholes]
    scratch += [quads, quads, quads, quads, held(8, rows, dtype=f32), held(QUADS, 8, rows, dtype=f32)]
    scratch += [own, own, own, held(rows // GRID_COLS + 6, 48, width, dtype=f32)]
    scratch += [sems(far), sems(far), sems(10), sems(BLOCKS), sems(BLOCKS), sems(BLOCKS)]
    scratch += [sems(CHUNKS, 3), sems(CHUNKS, 4)] + [sems(BLOCKS)] * 5
    scratch += [sems(2, width // 128)] * 4
    encoded, grad_tokens = pl.pallas_call(
        block_kernel,
        out_shape=[struct((rows, width))] * 2,
        in_specs=[pl.BlockSpec(memory_space=pltpu.SMEM)] + [ANY] * len(args),
        out_specs=[ANY] * 2,
        scratch_shapes=scratch,
        compiler_params=pltpu.CompilerParams(
            collective_id=1, has_side_effects=True, vmem_limit_bytes=WHOLE
        ),
    )(drop_seed, *args)
    alive = tissue[:, None] > 0
    nothing = jnp.zeros_like(encoded)
    return (jnp.where(alive, encoded, nothing), jnp.where(alive, grad_tokens, nothing))


def solution(mesh):
    placed = (
        P("ctx", "head"),
        P("ctx"),
        P(None, "head"),
        P("head"),
        P(),
        P(None, None, "head"),
        P("head", None),
        P(),
        P("ctx", "head"),
    )
    return jax.shard_map(
        on_device,
        mesh=mesh,
        in_specs=placed,
        out_specs=(P("ctx", "head"), P("ctx", "head")),
        check_vma=False,
    )
```

```python
import jax
import jax.numpy as jnp
from jax import lax
from jax.experimental import pallas as pl
from jax.experimental.pallas import tpu as pltpu
from jax.sharding import PartitionSpec as P

HEAD_DIM = 64
GRID_COLS = 32
ROWS = 128
QUADS = 4
BLOCKS = 16
SPAN = BLOCKS * ROWS
CHUNK = 512
HALF = ROWS // 2
WHOLE = 60 << 20
CHUNKS = SPAN // CHUNK
PER = CHUNK // ROWS
TILE = (3 * PER + 7) // 8 * 8

DROP_LEVEL = 103
KEEP_SCALE = 1024.0 / 921.0
NEG = -1e30
EPS = 1e-05
DEAD = 2.0**100

MESH = pl.DeviceIdType.MESH
ANY = pl.BlockSpec(memory_space=pl.ANY)
NT = (((1,), (1,)), ((), ()))


def struct(shape, dtype=jnp.bfloat16):
    return jax.ShapeDtypeStruct(shape, dtype)


def div(a, b):
    return lax.div(a, jnp.int32(b))


def mod(a, b):
    return lax.rem(a, jnp.int32(b))


def place():
    ctx = lax.axis_index("ctx")
    return ctx, div(ctx, 16), mod(div(ctx, 8), 2), mod(ctx, 8)


def query_peers():
    ctx, x, y, z = place()
    mine = mod(ctx, 16)
    peers = []
    for up, over in ((1, 4), (1, 3), (1, 5), (0, 4), (1, 2), (1, 6), (0, 3), (0, 5)) + (
        (1, 1), (1, 7), (0, 2), (0, 6), (1, 0), (0, 1), (0, 7)
    ):
        to_y, to_z = mod(y + up, 2), mod(z + over, 8)
        to = to_y * 8 + to_z
        peers.append((x * 16 + to, to, 2 * to_y + mod(to_z, 2)))
    return mine, 2 * y + mod(z, 2), peers


def key_peers():
    ctx, x, y, z = place()
    bit = mod(z, 2)
    mine = x * 4 + y * 2 + bit
    peers = []
    for side, up, over in ((2, 1, 1), (2, 1, 0), (1, 1, 1), (3, 1, 1), (1, 1, 0), (3, 1, 0)) + (
        (2, 0, 1), (0, 1, 1), (2, 0, 0), (0, 1, 0), (1, 0, 1), (3, 0, 1), (1, 0, 0), (3, 0, 0), (0, 0, 1)
    ):
        to_x, to_y, to_bit = mod(x + side, 4), mod(y + up, 2), mod(bit + over, 2)
        to = to_x * 4 + to_y * 2 + to_bit
        peers.append((to_x * 16 + to_y * 8 + z - bit + to_bit, to, to_y * 2 + to_bit))
    return mine, 2 * y + bit, peers


def stat_peers():
    ctx, x, y, z = place()
    mine = div(z, 2)
    base = ctx - z + mod(z, 2)
    peers = []
    for step in range(1, 4):
        to = mod(mine + step, 4)
        peers.append((base + to * 2, to))
    return mine, peers


def head_peers():
    mine = lax.axis_index("head")
    return mine, [mod(mine + step, 4) for step in range(1, 4)]


class Copies:
    def __init__(self, send, recv, own):
        self.send, self.recv, self.own = send, recv, own
        self.far, self.near = [], []

    def to(self, src, dst, device, recv=None):
        at = len(self.far)
        copy = pltpu.make_async_remote_copy(
            src_ref=src,
            dst_ref=dst,
            send_sem=self.send.at[at],
            recv_sem=self.recv.at[at] if recv is None else recv,
            device_id=device,
            device_id_type=MESH,
        )
        copy.start()
        self.far.append(copy)
        return copy

    def here(self, src, dst):
        copy = pltpu.make_async_copy(src, dst, self.own.at[len(self.near)])
        copy.start()
        self.near.append(copy)
        return copy

    def sent(self):
        for copy in self.far:
            copy.wait_send()


def received(copies):
    for copy in copies:
        copy.wait_recv()


def arriving(slot, send, recv, device):
    return pltpu.make_async_remote_copy(
        src_ref=slot,
        dst_ref=slot,
        send_sem=send,
        recv_sem=recv,
        device_id=device,
        device_id_type=MESH,
    )


def ring_ids():
    ctx = lax.axis_index("ctx")
    return mod(ctx + 63, 64), mod(ctx + 1, 64)


def everyone():
    ids = []
    for (q, _, _), (k, _, _) in zip(query_peers()[2], key_peers()[2]):
        ids += [{"ctx": q}, {"ctx": k}]
    before, after = ring_ids()
    return ids + [{"ctx": before}, {"ctx": after}] + [{"head": h} for h in head_peers()[1]]


class Halo:
    def __init__(self, field, above, below, send, recv):
        self.ctx = lax.axis_index("ctx")
        before, after = ring_ids()
        self.above, self.below = above, below
        self.down, self.up = [], []
        for tile in range(field.shape[1] // 128):
            cols = pl.ds(tile * 128, 128)
            for side, (rows, dst, to, list_) in enumerate(
                ((32, above, after, self.down), (0, below, before, self.up))
            ):
                list_.append(
                    pltpu.make_async_remote_copy(
                        src_ref=field.at[pl.ds(rows, 96), cols],
                        dst_ref=dst.at[:, cols],
                        send_sem=send.at[side, tile],
                        recv_sem=recv.at[side, tile],
                        device_id={"ctx": to},
                        device_id_type=MESH,
                    )
                )

    def clear(self):
        @pl.when(self.ctx == 0)
        def _():
            self.above[...] = jnp.zeros_like(self.above)

        @pl.when(self.ctx == 63)
        def _():
            self.below[...] = jnp.zeros_like(self.below)

    def start(self):
        @pl.when(self.ctx < 63)
        def _():
            for copy in self.down:
                copy.start()

        @pl.when(self.ctx > 0)
        def _():
            for copy in self.up:
                copy.start()

    def ready(self, tile):
        @pl.when(self.ctx > 0)
        def _():
            self.down[tile].wait_recv()

        @pl.when(self.ctx < 63)
        def _():
            self.up[tile].wait_recv()

    def sent(self):
        @pl.when(self.ctx < 63)
        def _():
            for copy in self.down:
                copy.wait_send()

        @pl.when(self.ctx > 0)
        def _():
            for copy in self.up:
                copy.wait_send()


def announce(ids):
    barrier = pltpu.get_barrier_semaphore()
    for device in ids:
        pl.semaphore_signal(barrier, inc=1, device_id=device, device_id_type=MESH)


def all_here(ids):
    pl.semaphore_wait(pltpu.get_barrier_semaphore(), len(ids))


def lanes(rows, width=128):
    return lax.broadcasted_iota(jnp.int32, (rows, width), 1)


def normalised(full_ref):
    parts = [full_ref[i].astype(jnp.float32) for i in range(QUADS)]
    width = QUADS * parts[0].shape[1]
    mean = sum(jnp.sum(p, axis=1, keepdims=True) for p in parts) / width
    parts = [p - mean for p in parts]
    var = sum(jnp.sum(p * p, axis=1, keepdims=True) for p in parts) / width
    spread = lax.rsqrt(var + EPS)
    return [p * spread for p in parts], spread


def fold(top, bottom, low_half):
    low = lanes(top.shape[0]) < HEAD_DIM
    if low_half:
        return jnp.where(low, top, pltpu.roll(bottom, 64, 1))
    return jnp.where(low, pltpu.roll(top, 64, 1), bottom)


def fold_rows(block, low_half):
    return fold(block[0:64], block[64:128], low_half)


def unfold_rows(packed, low_half):
    moved = pltpu.roll(packed, 64, 1)
    return jnp.concatenate([packed, moved] if low_half else [moved, packed], axis=0)


def query_chunk(q_ref, d_ref, at):
    blocks = []
    for block in range(PER):
        q = unfold_rows(q_ref[PER * at + block].astype(jnp.float32), False)
        d = unfold_rows(d_ref[PER * at + block].astype(jnp.float32), True)
        blocks.append(jnp.where(lanes(ROWS) < HEAD_DIM, d, q))
    return jnp.concatenate(blocks, axis=0)


def key_block(part):
    part = part.astype(jnp.float32)
    alive = part[:, 0:1] < DEAD / 2
    lane = lanes(ROWS)
    extra = jnp.where(lane == 0, jnp.where(alive, 0.0, NEG), jnp.where(lane < 4, 1.0, 0.0))
    return jnp.concatenate([jnp.where(alive, part, 0.0), extra], axis=1).astype(jnp.bfloat16)


def rows_at(start, count_, multiple):
    return pl.ds(pl.multiple_of(start, multiple), count_)


def scores_of(qd, keys):
    lane = lanes(qd.shape[0])
    left = jnp.concatenate(
        [jnp.where(lane >= HEAD_DIM, qd * 0.125, 0.0), jnp.where(lane == 0, 1.0, 0.0)], axis=1
    ).astype(jnp.bfloat16)
    return lax.dot_general(left, keys, NT, preferred_element_type=jnp.float32)


def forward_chunk(qd, keys, weights, rows, attended):
    lane = lanes(CHUNK)
    scores = scores_of(qd, keys[...])
    highest = jnp.max(scores, axis=1, keepdims=True)
    part = jnp.exp(scores - highest).astype(jnp.bfloat16)
    weights[rows, :] = part
    summed = jnp.dot(part, keys[...], preferred_element_type=jnp.float32)
    totals = summed[:, 129:130]
    mine = summed[:, 0:128] / totals
    attended[rows, :] = mine
    inner = jnp.sum(jnp.where(lane < HEAD_DIM, mine * qd, 0.0), axis=1, keepdims=True)
    log_total = highest + jnp.log(totals)
    table = jnp.where(
        lane == 0, log_total, jnp.where(lane == 1, inner, jnp.where(lane == 2, highest, 0.0))
    ).T
    parts = [table[k : k + 1, h * ROWS : (h + 1) * ROWS] for k in range(3) for h in range(PER)]
    return jnp.concatenate(parts + [jnp.zeros((TILE - 3 * PER, 128), jnp.float32)], axis=0)


def chunk_columns(stats, mine):
    logs = [stats[i][0:PER] for i in range(4)]
    top = jnp.maximum(jnp.maximum(logs[0], logs[1]), jnp.maximum(logs[2], logs[3]))
    total = top + jnp.log(sum(jnp.exp(part - top) for part in logs))
    shift = sum(jnp.exp(logs[i] - total) * stats[i][PER : 2 * PER] for i in range(4))
    share = jnp.exp(mine[0:PER] - total)
    factor = jnp.exp(mine[2 * PER : 3 * PER] - total)
    rest = jnp.zeros((128 - 3 * PER, 128), jnp.float32)
    rows = jnp.concatenate([share, shift, factor, rest], axis=0).T
    return [
        jnp.concatenate([rows[:, k * PER + h : k * PER + h + 1] for h in range(PER)], axis=0)
        for k in range(3)
    ]


def backward_chunk(qd, keys, weights, shift, factor, value_acc, key_acc):
    lane = lanes(CHUNK)
    high = shift.astype(jnp.bfloat16).astype(jnp.float32)
    middle = (shift - high).astype(jnp.bfloat16).astype(jnp.float32)
    low = shift - high - middle
    extra = jnp.where(
        lane == 1, -high, jnp.where(lane == 2, -middle, jnp.where(lane == 3, -low, 0.0))
    )
    left = jnp.concatenate([jnp.where(lane < HEAD_DIM, qd, 0.0), extra], axis=1)
    dprob = lax.dot_general(
        left.astype(jnp.bfloat16), keys[...], NT, preferred_element_type=jnp.float32
    )
    slope = (weights.astype(jnp.float32) * dprob).astype(jnp.bfloat16)
    query_grad = jnp.dot(slope, keys[:, 0:128], preferred_element_type=jnp.float32)
    scaled = (qd * factor * jnp.where(lane < HEAD_DIM, 1.0, 0.125)).T.astype(jnp.bfloat16)
    value_acc[...] += jnp.dot(scaled[0:64], weights, preferred_element_type=jnp.float32)
    key_acc[...] += jnp.dot(scaled[64:128], slope, preferred_element_type=jnp.float32)
    return query_grad * (factor * 0.125)


def keep_mask(anchor, counter, row_ids, col_ids):
    mixed = (
        row_ids * jnp.int32(374761393)
        + col_ids * jnp.int32(668265263)
        + anchor * jnp.int32(1274126177)
        + counter
    )
    mixed = jnp.bitwise_xor(mixed, lax.shift_right_logical(mixed, jnp.full_like(mixed, 15)))
    mixed = mixed * jnp.int32(16777619)
    mixed = jnp.bitwise_xor(mixed, lax.shift_right_logical(mixed, jnp.full_like(mixed, 13)))
    mixed = mixed * jnp.int32(1274126177)
    mixed = jnp.bitwise_xor(mixed, lax.shift_right_logical(mixed, jnp.full_like(mixed, 16)))
    return (jnp.bitwise_and(mixed, jnp.int32(1023)) >= DROP_LEVEL).astype(jnp.float32)


def own_keep(seed_ref, rows, width):
    row_ids = lax.axis_index("ctx") * rows + lax.broadcasted_iota(jnp.int32, (rows, width), 0)
    col_ids = lax.axis_index("head") * width + lax.broadcasted_iota(jnp.int32, (rows, width), 1)
    return keep_mask(seed_ref[0], seed_ref[1], row_ids, col_ids)


def alive_column(tissue_ref):
    row = tissue_ref[...].astype(jnp.float32)
    return jnp.broadcast_to(row, (ROWS, ROWS)).T


def merged_tap(taps_ref, row, col, cols):
    tap = taps_ref[row * 7 + col : row * 7 + col + 1, cols]
    if 1 <= row <= 5 and 1 <= col <= 5:
        at = 49 + (row - 1) * 5 + col - 1
        tap = tap + taps_ref[at : at + 1, cols]
    if 2 <= row <= 4 and 2 <= col <= 4:
        at = 74 + (row - 2) * 3 + col - 2
        tap = tap + taps_ref[at : at + 1, cols]
    return tap


def depthwise(flipped, field_ref, halo, taps_ref, bias, padded):
    width = field_ref.shape[1]
    grid_rows = ROWS // GRID_COLS
    padded[3:7, 8:40, :] = field_ref[...].astype(jnp.float32).reshape(grid_rows, GRID_COLS, width)
    for tile in range(width // 128):
        cols = slice(tile * 128, tile * 128 + 128)
        total = padded[3:7, 8:40, cols]
        if bias is not None:
            total = total + bias[:, cols].reshape(1, 1, 128)
        halo.ready(tile)
        for start, ref in ((0, halo.above), (7, halo.below)):
            part = ref[:, cols].astype(jnp.float32)
            padded[start : start + 3, 8:40, cols] = part.reshape(3, GRID_COLS, 128)
        for col in range(7):
            moved = padded[:, 5 + col : 37 + col, cols]
            for row in range(7):
                if flipped:
                    tap = merged_tap(taps_ref, 6 - row, 6 - col, cols)
                else:
                    tap = merged_tap(taps_ref, row, col, cols)
                total = total + tap.reshape(1, 1, 128) * moved[row : row + grid_rows]
        yield cols, total.reshape(ROWS, 128)


def block_kernel(
    seed_ref,
    tokens_in,
    tissue_in,
    grad_in,
    taps_in,
    bias_in,
    gain_in,
    w_in,
    w_out_in,
    encoded_out,
    tokens_out,
    tokens,
    tissue,
    grad,
    taps,
    bias,
    gain,
    w,
    w_out,
    keep,
    masked,
    above,
    below,
    above_back,
    below_back,
    drop_full,
    full,
    query_part,
    grad_part,
    key_part,
    query_all,
    grad_all,
    key_all,
    keys,
    weights,
    attended,
    stats,
    value_acc,
    key_acc,
    query_out,
    out_out,
    key_out,
    query_back,
    out_back,
    key_back,
    grad_send,
    grad_recv,
    branch_send,
    branch_recv,
    sums_send,
    sums_recv,
    source,
    encoded,
    result,
    padded,
    send,
    recv,
    own,
    query_recv,
    grad_sem,
    key_recv,
    stat_send,
    stat_recv,
    query_back_send,
    query_back_recv,
    out_back_send,
    out_back_recv,
    key_back_recv,
    halo_send,
    halo_recv,
    halo_back_send,
    halo_back_recv,
):
    rows, width = tokens.shape
    ids = everyone()
    announce(ids)
    copies = Copies(send, recv, own)
    first = [
        copies.here(src, dst)
        for src, dst in ((tokens_in, tokens), (tissue_in, tissue), (grad_in, grad))
    ]
    for_conv = [copies.here(taps_in, taps), copies.here(bias_in, bias)]
    for_grad = [copies.here(w_out_in, w_out)]
    for_project = [copies.here(gain_in, gain), copies.here(w_in, w)]
    mine, heads = head_peers()
    q_mine, slot, q_peers = query_peers()
    k_mine, _, k_peers = key_peers()
    s_mine, s_peers = stat_peers()
    query_base = lax.axis_index("ctx") - q_mine
    halo = Halo(masked, above, below, halo_send, halo_recv)
    halo_back = Halo(source, above_back, below_back, halo_back_send, halo_back_recv)
    halo.clear()
    halo_back.clear()
    padded[:, 0:8, :] = jnp.zeros((padded.shape[0], 8, width), jnp.float32)
    padded[:, 40:48, :] = jnp.zeros((padded.shape[0], 8, width), jnp.float32)
    keep[...] = own_keep(seed_ref, rows, width)
    for copy in first:
        copy.wait()
    alive = alive_column(tissue)
    column = alive[:, 0:1]
    masked[...] = (tokens[...].astype(jnp.float32) * column).astype(jnp.bfloat16)
    all_here(ids)
    halo.start()
    upstream = grad[...].astype(jnp.float32) * column
    drop_full[mine] = (upstream * keep[...] * KEEP_SCALE).astype(jnp.bfloat16)
    drops = [copies.to(drop_full.at[mine], drop_full.at[mine], {"head": h}) for h in heads]

    for copy in for_conv:
        copy.wait()
    for cols, part in depthwise(False, masked, halo, taps, bias[...].reshape(1, width), padded):
        full[mine, :, cols] = (part * alive).astype(jnp.bfloat16)
    parts = [copies.to(full.at[mine], full.at[mine], {"head": h}) for h in heads]

    for copy in for_grad:
        copy.wait()
    received(drops)
    out_grad = sum(
        lax.dot_general(
            drop_full[i],
            w_out[:, i * width : (i + 1) * width],
            NT,
            preferred_element_type=jnp.float32,
        )
        for i in range(QUADS)
    )
    for j in range(QUADS):
        pair = out_grad[:, 128 * (j // 2) : 128 * (j // 2) + 128]
        grad_part[j] = fold_rows(pair, j % 2 == 0).astype(jnp.bfloat16)
    for c, _, h in q_peers:
        copies.to(grad_part.at[h], grad_all.at[q_mine], {"ctx": c}, grad_sem.at[q_mine])
    grad_all[q_mine] = grad_part[slot]

    for copy in for_project:
        copy.wait()
    received(parts)
    unit, _ = normalised(full)
    gain_row = gain[...].reshape(1, QUADS * width)
    sums = [jnp.zeros((rows, w.shape[2]), jnp.float32) for _ in range(3)]
    for i in range(QUADS):
        span = slice(i * width, (i + 1) * width)
        normed = (unit[i] * gain_row[:, span]).astype(jnp.bfloat16)
        for k in range(3):
            sums[k] = sums[k] + jnp.dot(normed, w[k, span, :], preferred_element_type=jnp.float32)
    low = lanes(ROWS) < HEAD_DIM
    dead = alive == 0.0
    for j in range(QUADS):
        q, k, v = (part[:, 128 * (j // 2) : 128 * (j // 2) + 128] for part in sums)
        query_part[j] = fold_rows(q, j % 2 == 0).astype(jnp.bfloat16)
        if j % 2 == 0:
            both = jnp.where(low, v, pltpu.roll(k, 64, 1))
        else:
            both = jnp.where(low, pltpu.roll(v, 64, 1), k)
        key_part[j] = jnp.where(dead, DEAD, both).astype(jnp.bfloat16)
    for c, _, h in k_peers:
        copies.to(key_part.at[h], key_all.at[k_mine], {"ctx": c}, key_recv.at[k_mine])
    for c, _, h in q_peers:
        copies.to(query_part.at[h], query_all.at[q_mine], {"ctx": c}, query_recv.at[q_mine])
    query_all[q_mine] = query_part[slot]
    keys[rows_at(k_mine * ROWS, ROWS, ROWS), :] = key_block(key_part[slot])
    value_acc[...] = jnp.zeros_like(value_acc)
    key_acc[...] = jnp.zeros_like(key_acc)
    for c, at, _ in k_peers:
        arriving(key_all.at[at], send.at[0], key_recv.at[at], {"ctx": c}).wait_recv()
        keys[rows_at(at * ROWS, ROWS, ROWS), :] = key_block(key_all[at])

    def chunk_at(step):
        return mod(div(q_mine, PER) + 1 + step, CHUNKS)

    def forward_step(step, _):
        chunk = chunk_at(step)
        for half in range(PER):
            at = PER * chunk + half

            @pl.when(at != q_mine)
            def _(at=at):
                peer = {"ctx": query_base + at}
                arriving(grad_all.at[at], send.at[0], grad_sem.at[at], peer).wait_recv()
                arriving(query_all.at[at], send.at[0], query_recv.at[at], peer).wait_recv()

        qd = query_chunk(query_all, grad_all, chunk)
        stats[chunk, s_mine] = forward_chunk(
            qd, keys, weights, rows_at(chunk * CHUNK, CHUNK, CHUNK), attended
        )
        for i, (c, _) in enumerate(s_peers):
            pltpu.make_async_remote_copy(
                src_ref=stats.at[chunk, s_mine],
                dst_ref=stats.at[chunk, s_mine],
                send_sem=stat_send.at[chunk, i],
                recv_sem=stat_recv.at[chunk, s_mine],
                device_id={"ctx": c},
                device_id_type=MESH,
            ).start()
        return 0

    lax.fori_loop(0, CHUNKS, forward_step, 0)

    def backward_step(step, _):
        chunk = chunk_at(step)
        for c, at in s_peers:
            arriving(
                stats.at[chunk, at], send.at[0], stat_recv.at[chunk, at], {"ctx": c}
            ).wait_recv()
        share, shift, factor = chunk_columns(
            [stats[chunk, i] for i in range(4)], stats[chunk, s_mine]
        )
        qd = query_chunk(query_all, grad_all, chunk)
        rows_ = rows_at(chunk * CHUNK, CHUNK, CHUNK)
        query_grad = backward_chunk(
            qd, keys, weights[rows_, :], shift, factor, value_acc, key_acc
        )
        out = attended[rows_, :] * share
        for half in range(PER):
            at = PER * chunk + half
            span = slice(half * ROWS, (half + 1) * ROWS)
            query_out[at] = fold_rows(query_grad[span], False).astype(jnp.bfloat16)
            out_out[at] = fold_rows(out[span], True).astype(jnp.bfloat16)

            @pl.when(at != q_mine)
            def _(at=at):
                for src, dst, sent, got in (
                    (query_out, query_back, query_back_send, query_back_recv),
                    (out_out, out_back, out_back_send, out_back_recv),
                ):
                    pltpu.make_async_remote_copy(
                        src_ref=src.at[at],
                        dst_ref=dst.at[q_mine],
                        send_sem=sent.at[at],
                        recv_sem=got.at[q_mine],
                        device_id={"ctx": query_base + at},
                        device_id_type=MESH,
                    ).start()

        return 0

    lax.fori_loop(0, CHUNKS, backward_step, 0)
    def key_rows(at):
        cols = rows_at(at * ROWS, ROWS, ROWS)
        both = jnp.concatenate([value_acc[:, cols], key_acc[:, cols]], axis=0)
        return both.T.astype(jnp.bfloat16)

    for c, at, _ in k_peers:
        key_out[at] = key_rows(at)
        copies.to(key_out.at[at], key_back.at[k_mine], {"ctx": c}, key_back_recv.at[k_mine])
    key_back[k_mine] = key_rows(k_mine)
    query_back[q_mine] = query_out[q_mine]
    out_back[q_mine] = out_out[q_mine]

    def total(ref, slots):
        parts = [ref[s].astype(jnp.float32) for s in slots]
        return (parts[0] + parts[1]) + (parts[2] + parts[3])

    def queries(ref):
        heads_ = []
        for j in range(QUADS):
            packed = total(ref, [8 * (j // 2) + 2 * k + j % 2 for k in range(4)])
            heads_.append(unfold_rows(packed, j % 2 == 0))
        pairs = [jnp.where(low, heads_[2 * p], heads_[2 * p + 1]) for p in range(2)]
        return jnp.concatenate(pairs, axis=1).astype(jnp.bfloat16)

    unit, spread = normalised(full)
    for c, at, _ in q_peers:
        arriving(out_back.at[at], send.at[0], out_back_recv.at[at], {"ctx": c}).wait_recv()
    out = queries(out_back)
    for i in range(QUADS):
        span = slice(i * width, (i + 1) * width)
        branch_send[i] = jnp.dot(
            out, w_out[:, span], preferred_element_type=jnp.float32
        ).astype(jnp.bfloat16)
    branches = [copies.to(branch_send.at[h], branch_recv.at[mine], {"head": h}) for h in heads]
    branch_recv[mine] = branch_send[mine]

    for c, at, _ in q_peers:
        arriving(query_back.at[at], send.at[0], query_back_recv.at[at], {"ctx": c}).wait_recv()
    query_sum = queries(query_back)
    for c, at, _ in k_peers:
        arriving(key_back.at[at], send.at[0], key_back_recv.at[at], {"ctx": c}).wait_recv()
    both = [total(key_back, [4 * k + j for k in range(4)]) for j in range(QUADS)]
    value_sum = [jnp.where(low, both[2 * p], pltpu.roll(both[2 * p + 1], 64, 1)) for p in range(2)]
    key_sum = [jnp.where(low, pltpu.roll(both[2 * p], 64, 1), both[2 * p + 1]) for p in range(2)]
    grads = [
        query_sum,
        jnp.concatenate(key_sum, axis=1).astype(jnp.bfloat16),
        jnp.concatenate(value_sum, axis=1).astype(jnp.bfloat16),
    ]
    plain = jnp.zeros((ROWS, 1), jnp.float32)
    crossed = jnp.zeros((ROWS, 1), jnp.float32)
    for i in range(QUADS):
        span = slice(i * width, (i + 1) * width)
        part = sum(
            lax.dot_general(grads[k], w[k, span, :], NT, preferred_element_type=jnp.float32)
            for k in range(3)
        )
        grad_send[i] = part.astype(jnp.bfloat16)
        scaled = part * gain_row[:, span]
        plain = plain + jnp.sum(scaled, axis=1, keepdims=True)
        crossed = crossed + jnp.sum(scaled * unit[i], axis=1, keepdims=True)
    lane = lanes(ROWS)
    sums_send[...] = jnp.where(lane == 0, plain, jnp.where(lane == 1, crossed, 0.0)).T[0:8]
    scattered = []
    for h in heads:
        scattered.append(copies.to(grad_send.at[h], grad_recv.at[mine], {"head": h}))
        scattered.append(copies.to(sums_send, sums_recv.at[mine], {"head": h}))
    grad_recv[mine] = grad_send[mine]
    sums_recv[mine] = sums_send[...]

    own_unit = jnp.zeros((ROWS, width), jnp.float32)
    own_gain = jnp.zeros((1, width), jnp.float32)
    for i in range(QUADS):
        own_unit = jnp.where(mine == i, unit[i], own_unit)
        own_gain = jnp.where(mine == i, gain_row[:, i * width : (i + 1) * width], own_gain)
    received(scattered)
    means = (sums_recv[0] + sums_recv[1]) + (sums_recv[2] + sums_recv[3])
    means = jnp.concatenate([means, jnp.zeros((120, 128), jnp.float32)], axis=0).T / (QUADS * width)
    scaled = total(grad_recv, range(QUADS)) * own_gain
    inner = scaled - means[:, 0:1] - own_unit * means[:, 1:2]
    column = alive_column(tissue)[:, 0:1]
    upstream = grad[...].astype(jnp.float32) * column
    source[...] = ((upstream + inner * spread) * column).astype(jnp.bfloat16)
    halo_back.start()
    received(branches)
    branch = total(branch_recv, range(QUADS))
    residual = full[mine].astype(jnp.float32)
    encoded[...] = (residual + branch * keep[...] * KEEP_SCALE).astype(jnp.bfloat16)
    outs = [copies.here(encoded, encoded_out)]
    for cols, part in depthwise(True, source, halo_back, taps, None, padded):
        result[:, cols] = part.astype(jnp.bfloat16)
    outs.append(copies.here(result, tokens_out))

    halo.sent()
    halo_back.sent()
    copies.sent()
    for chunk in range(CHUNKS):
        for i, (c, _) in enumerate(s_peers):
            tile = stats.at[chunk, s_mine]
            arriving(tile, stat_send.at[chunk, i], stat_recv.at[chunk, s_mine], {"ctx": c}).wait_send()
    for c, at, _ in q_peers:
        peer = {"ctx": c}
        arriving(query_out.at[at], query_back_send.at[at], query_back_recv.at[at], peer).wait_send()
        arriving(out_out.at[at], out_back_send.at[at], out_back_recv.at[at], peer).wait_send()
    for copy in outs:
        copy.wait()


def on_device(tokens, tissue, conv_taps, conv_bias, ln_gain, w_qkv, w_out, drop_seed, grad_out):
    rows, width = tokens.shape
    args = [
        tokens,
        tissue[None, :],
        grad_out,
        conv_taps,
        conv_bias,
        ln_gain,
        w_qkv.transpose(1, 0, 2),
        w_out,
    ]
    far = 3 + 15 + 3 + 15 + 15 + 15 + 3 + 6

    def held(*shape, dtype=jnp.bfloat16):
        return pltpu.VMEM(shape, dtype)

    def sems(*shape):
        return pltpu.SemaphoreType.DMA(shape)

    f32 = jnp.float32
    quads = held(QUADS, rows, width)
    halves = held(BLOCKS, HALF, 128)
    wholes = held(BLOCKS, ROWS, 128)
    halo = held(96, width)
    own = held(rows, width)
    scratch = [pltpu.VMEM(a.shape, a.dtype) for a in args]
    scratch += [held(rows, width, dtype=f32), own, halo, halo, halo, halo, quads, quads]
    scratch += [held(QUADS, HALF, 128), held(QUADS, HALF, 128), held(QUADS, ROWS, 128)]
    scratch += [halves, halves, wholes, held(SPAN, 256), held(SPAN, SPAN)]
    scratch += [held(SPAN, 128, dtype=f32), held(CHUNKS, 4, TILE, 128, dtype=f32)]
    scratch += [held(HEAD_DIM, SPAN, dtype=f32), held(HEAD_DIM, SPAN, dtype=f32)]
    scratch += [halves, halves, wholes, halves, halves, wholes]
    scratch += [quads, quads, quads, quads, held(8, rows, dtype=f32), held(QUADS, 8, rows, dtype=f32)]
    scratch += [own, own, own, held(rows // GRID_COLS + 6, 48, width, dtype=f32)]
    scratch += [sems(far), sems(far), sems(10), sems(BLOCKS), sems(BLOCKS), sems(BLOCKS)]
    scratch += [sems(CHUNKS, 3), sems(CHUNKS, 4)] + [sems(BLOCKS)] * 5
    scratch += [sems(2, width // 128)] * 4
    encoded, grad_tokens = pl.pallas_call(
        block_kernel,
        out_shape=[struct((rows, width))] * 2,
        in_specs=[pl.BlockSpec(memory_space=pltpu.SMEM)] + [ANY] * len(args),
        out_specs=[ANY] * 2,
        scratch_shapes=scratch,
        compiler_params=pltpu.CompilerParams(
            collective_id=1, has_side_effects=True, vmem_limit_bytes=WHOLE
        ),
    )(drop_seed, *args)
    alive = tissue[:, None] > 0
    nothing = jnp.zeros_like(encoded)
    return (jnp.where(alive, encoded, nothing), jnp.where(alive, grad_tokens, nothing))


def solution(mesh):
    placed = (
        P("ctx", "head"),
        P("ctx"),
        P(None, "head"),
        P("head"),
        P(),
        P(None, None, "head"),
        P("head", None),
        P(),
        P("ctx", "head"),
    )
    return jax.shard_map(
        on_device,
        mesh=mesh,
        in_specs=placed,
        out_specs=(P("ctx", "head"), P("ctx", "head")),
        check_vma=False,
    )
```
